32 devices in a mesh: space: 4 (over z), band: 8 (over y, x, core).
Axes of the slice: x: 2, y: 2, z: 4, core: 2. Of those that a mesh axis runs over, the one named last changes fastest.
Arguments:
- wavefunctions: bfloat16 [256, 5120], P('band', 'space'), may hold values from -6 to 6
- cell_hamiltonian: bfloat16 [36, 216, 216], P('space'), may hold values from -1 to 2.25, as said below
- connectivity: int32 [36, 216], P('space'), may hold values from 0 to 1535, as said below
- face_nodes: int32 [1024], P('space'), may hold values from 0 to 1279, as said below
- basis_values: bfloat16 [216, 343], replicated, may hold values from -0.4375 to 0.4375
- quad_weights: float32 [36, 343], P('space'), may hold values from 0.1 to 1
- core_density: float32 [36, 343], P('space'), may hold values from 0.05 to 2
- occupancy: float32 [256], P('band'), may hold values from 0.1 to 1
- ritz_values: float32 [256], P('band'), may hold values from -1 to 6
Outputs:
- residual: float32 [256, 5120], P('band', 'space')
- potential: float32 [36, 343], P('space')
The draws below stay inside these ranges and needn't reach their ends.
Inputs may be any that keep to these rules, and one draw needn't show every extreme that they name: `connectivity`: block s of 9 rows belongs to domain s and names each cell's 216 distinct nodes in that domain's extended numbering: values below 256 are its ghost columns, 256 + n is its owned node n. A domain's cells come in 1 layer of 9 rows; only the first layer names ghost columns and only the last layer names nodes listed in face_nodes. Every ghost column and every owned node is named by some cell. `face_nodes`: block s of 256 entries lists distinct owned nodes of domain s, in the order in which domain s + 1 numbers its ghost columns. `cell_hamiltonian`: each cell's matrix is symmetric.
All inputs are finite; a program needn't handle non-finite values.
Results may differ from the reference program's by a relative error of at most 0.0024.
Values may be sent and summed in bfloat16 or wider, within the bound.
No kernel may reach another device: no remote copies, remote signals or barrier semaphores. Data moves between devices by JAX's collectives and lax.ppermute only.
A program may use at most 64 MiB of HBM per device.

```python
import math
import jax
import jax.numpy as jnp
from jax import lax

BASIS_ORDER = 5
LAYER_SIDE = 3
SLAB_THICKNESS = 1
WF_DEV = 32
CELL_NODES = 216
QUAD = 343
BORDER_VERTICES = 256
CELL_DEV = 9
PATCH_VERTICES = 1280
CELLS = 36
NODES = 5120
NWF = 256
N_SPACE = 4
N_BAND = 8


def layout_tables(key):
    layout_key = jax.random.fold_in(key, 11)
    plane_side = LAYER_SIDE * BASIS_ORDER + 1
    order_next = BASIS_ORDER + 1
    domains = CELLS // CELL_DEV
    local_nodes = jnp.arange(CELL_NODES, dtype=jnp.int32)
    offset_depth = local_nodes // (order_next * order_next)
    offset_row = local_nodes // order_next % order_next
    offset_column = local_nodes % order_next

    def one_domain(partition_seed_handle):
        vertex_permutation_map = jax.random.permutation(jax.random.fold_in(partition_seed_handle, 1), PATCH_VERTICES).astype(jnp.int32)
        layer_order = jax.random.permutation(jax.random.fold_in(partition_seed_handle, 2), LAYER_SIDE * LAYER_SIDE).astype(jnp.int32)
        cell_index = jnp.arange(CELL_DEV, dtype=jnp.int32)
        layer_of = cell_index // (LAYER_SIDE * LAYER_SIDE)
        within = layer_order[cell_index % (LAYER_SIDE * LAYER_SIDE)]
        cell_row = within // LAYER_SIDE
        cell_column = within % LAYER_SIDE
        vertex_slab_position = BASIS_ORDER * layer_of[:, None] + offset_depth[None, :]
        node_row = BASIS_ORDER * cell_row[:, None] + offset_row[None, :]
        node_column = BASIS_ORDER * cell_column[:, None] + offset_column[None, :]
        interface_vertex_position = node_row * plane_side + node_column
        interior_vertex_position = jnp.maximum(vertex_slab_position - 1, 0) * BORDER_VERTICES + interface_vertex_position
        mesh_vertex_incidence = jnp.where(vertex_slab_position == 0, interface_vertex_position, BORDER_VERTICES + vertex_permutation_map[interior_vertex_position])
        border_vertex_indices = vertex_permutation_map[(SLAB_THICKNESS * BASIS_ORDER - 1) * BORDER_VERTICES + jnp.arange(BORDER_VERTICES, dtype=jnp.int32)]
        return (mesh_vertex_incidence.astype(jnp.int32), border_vertex_indices.astype(jnp.int32))
    domain_keys = jax.random.split(layout_key, domains)
    mesh_vertex_incidence, border_vertex_indices = jax.vmap(one_domain)(domain_keys)
    return (mesh_vertex_incidence.reshape(CELLS, CELL_NODES), border_vertex_indices.reshape(domains * BORDER_VERTICES))


def draw_connectivity(key, part):
    return layout_tables(key)[0]


def draw_face_nodes(key, part):
    return layout_tables(key)[1]


def draw_cell_hamiltonian(key, part):
    first_key = jax.random.fold_in(key, 21)
    second_key = jax.random.fold_in(key, 22)
    full_shape = (CELLS, CELL_NODES, CELL_NODES)
    raw_entries = jnp.clip(jax.random.normal(first_key, full_shape, jnp.float32), -4.0, 4.0)
    coupling = (raw_entries + jnp.swapaxes(raw_entries, 1, 2)) * (0.5 / math.sqrt(2.0 * CELL_NODES))
    diagonal = jax.random.uniform(second_key, (CELLS, CELL_NODES), jnp.float32, 0.3, 1.2)
    identity_matrix = jnp.eye(CELL_NODES, dtype=jnp.float32)
    return (coupling + diagonal[:, :, None] * identity_matrix[None]).astype(jnp.bfloat16)


def steps_of(stream_key, shape, cuts, least, top_value):
    level, own = 1.0, jax.random.fold_in(stream_key, 6)
    for dim, parts in cuts:
        steps = jnp.exp(jax.random.uniform(jax.random.fold_in(own, dim), (parts,), jnp.float32, least / len(cuts), top_value / len(cuts)))
        level = level * jnp.repeat(steps, shape[dim] // parts).reshape([-1 if axis == dim else 1 for axis in range(len(shape))])
    return level


def centred(rng, shape, scale, reach, shards=(), held_as=jnp.bfloat16):
    factor_of = steps_of(rng, shape, shards, -0.22, 0.18) if shards else 1.0
    values = jax.random.normal(rng, shape, jnp.float32) * scale * factor_of
    return jnp.minimum(jnp.maximum(values, -reach), reach).astype(held_as)


def setup_inputs(seed: int = 0) -> dict:
    key_list = jax.random.split(jax.random.key(seed), 10)
    wavefunctions = centred(key_list[0], (NWF, NODES), 1.0, 6.0, ((0, 8), (1, 4)))
    cell_hamiltonian = draw_cell_hamiltonian(jax.random.fold_in(key_list[9], 71), 0)
    connectivity = draw_connectivity(jax.random.fold_in(key_list[9], 71), 0)
    face_nodes = draw_face_nodes(jax.random.fold_in(key_list[9], 71), 0)
    basis_values = centred(key_list[4], (CELL_NODES, QUAD), CELL_NODES ** -0.5, 0.4375)
    quad_weights = jnp.clip(jnp.exp(math.log(1.0) - 2.3025851 * jax.random.uniform(key_list[5], (CELLS, QUAD), jnp.float32) ** steps_of(key_list[5], (CELLS, QUAD), ((0, 4),), -0.2, 0.2)), 0.1, 1.0)
    core_density = jnp.clip(jnp.exp(math.log(2.0) - 3.6888794 * jax.random.uniform(key_list[6], (CELLS, QUAD), jnp.float32) ** steps_of(key_list[6], (CELLS, QUAD), ((0, 4),), -0.2, 0.2)), 0.05, 2.0)
    occupancy = jnp.clip(jnp.exp(math.log(1.0) - 2.3025851 * jax.random.uniform(key_list[7], (NWF,), jnp.float32) ** steps_of(key_list[7], (NWF,), ((0, 8),), -0.2, 0.2)), 0.1, 1.0)
    ritz_values = jnp.clip(-1.0 + 7.0 * jax.random.uniform(key_list[8], (NWF,), jnp.float32) ** steps_of(key_list[8], (NWF,), ((0, 8),), -0.2, 0.2), -1.0, 6.0)
    return dict(wavefunctions=wavefunctions, cell_hamiltonian=cell_hamiltonian, connectivity=connectivity, face_nodes=face_nodes, basis_values=basis_values, quad_weights=quad_weights, core_density=core_density, occupancy=occupancy, ritz_values=ritz_values)


spectrum_center = 5.0
spectrum_half = 5.5


def exchange_correlation(density):
    radius = jnp.cbrt(0.75 / math.pi / density)
    exchange_part = -jnp.cbrt(3.0 / math.pi * density)
    shifted_radius = radius + 7.8
    correlation_part = -0.44 / shifted_radius - 0.44 * radius / (3.0 * shifted_radius * shifted_radius)
    return exchange_part + correlation_part


def pick_faces(owned_block, face_index):
    return owned_block[:, face_index]


def extend(values, face_nodes):
    wave_count = values.shape[0]
    owned = values.reshape(wave_count, N_SPACE, PATCH_VERTICES).transpose(1, 0, 2)
    face_values = jax.vmap(pick_faces)(owned, face_nodes.reshape(N_SPACE, BORDER_VERTICES))
    ghosts = jnp.concatenate([jnp.zeros_like(face_values[:1]), face_values[:-1]], axis=0)
    return jnp.concatenate([ghosts, owned], axis=2).astype(jnp.bfloat16)


def domain_cells(extended, domain_links):
    wave_count = extended.shape[0]
    gathered = jnp.take(extended, domain_links.reshape(-1), axis=1)
    return lax.optimization_barrier(gathered).reshape(wave_count, CELL_DEV, CELL_NODES)


def cell_products(cell_values, hamiltonian):
    return jnp.einsum("wcb,cab->wca", cell_values.astype(jnp.float32), hamiltonian)


def scatter_domain(contributions, domain_links):
    wave_count = contributions.shape[0]
    initial = jnp.zeros((wave_count, BORDER_VERTICES + PATCH_VERTICES), jnp.float32)
    return initial.at[:, domain_links.reshape(-1)].add(contributions.reshape(wave_count, -1))


def add_faces(owned_block, face_index, incoming):
    return owned_block.at[:, face_index].add(incoming)


def assemble(contributions, links_all, face_nodes):
    wave_count = contributions.shape[1]
    extended = jax.vmap(scatter_domain)(contributions, links_all)
    owned = extended[:, :, BORDER_VERTICES:]
    returned = jnp.concatenate([extended[1:, :, :BORDER_VERTICES], jnp.zeros_like(extended[:1, :, :BORDER_VERTICES])], axis=0)
    owned = jax.vmap(add_faces)(owned, face_nodes.reshape(N_SPACE, BORDER_VERTICES), returned)
    return owned.transpose(1, 0, 2).reshape(wave_count, NODES)


def reference(wavefunctions, cell_hamiltonian, connectivity, face_nodes, basis_values, quad_weights, core_density, occupancy, ritz_values):
    hamiltonian = cell_hamiltonian.astype(jnp.float32).reshape(N_SPACE, CELL_DEV, CELL_NODES, CELL_NODES)
    links_all = connectivity.reshape(N_SPACE, CELL_DEV, CELL_NODES)
    shape_values = basis_values.astype(jnp.float32)

    def cells_of(values):
        return jax.vmap(domain_cells)(extend(values, face_nodes), links_all)

    def apply_plain(values):
        return assemble(jax.vmap(cell_products)(cells_of(values), hamiltonian), links_all, face_nodes)

    def interpolate(cell_values):
        return jnp.einsum("swca,aq->swcq", cell_values.astype(jnp.float32), shape_values)

    def first_pass(totals, inputs):
        wave_block, weights = inputs
        starting = wave_block.astype(jnp.float32)
        term_one = (apply_plain(wave_block) - spectrum_center * starting) * (1.0 / spectrum_half)
        term_two = (apply_plain(term_one) - spectrum_center * term_one) * (2.0 / spectrum_half) - starting
        term_three = (apply_plain(term_two) - spectrum_center * term_two) * (2.0 / spectrum_half) - term_one
        values_at = interpolate(cells_of(term_three))
        totals = totals + jnp.sum(weights[None, :, None, None] * (values_at * values_at), axis=1)
        return totals, term_three

    wave_blocks = wavefunctions.reshape(N_BAND, WF_DEV, NODES)
    weight_blocks = occupancy.reshape(N_BAND, WF_DEV)
    initial = jnp.zeros((N_SPACE, CELL_DEV, QUAD), jnp.float32)
    totals, thirds = lax.scan(first_pass, initial, (wave_blocks, weight_blocks))
    density = core_density.reshape(N_SPACE, CELL_DEV, QUAD) + (2.0 / NWF) * totals
    potential = exchange_correlation(density)
    scaled_potential = quad_weights.reshape(N_SPACE, CELL_DEV, QUAD) * potential

    def second_pass(inputs):
        term_three, ritz_block = inputs
        cell_values = cells_of(term_three)
        products = jax.vmap(cell_products)(cell_values, hamiltonian)
        weighted = (interpolate(cell_values) * scaled_potential[:, None]).astype(jnp.bfloat16)
        weighted = lax.optimization_barrier(weighted)
        projected = jnp.einsum("swcq,aq->swca", weighted.astype(jnp.float32), shape_values)
        applied = assemble(products + projected, links_all, face_nodes)
        return applied - ritz_block[:, None] * term_three

    residual = lax.map(second_pass, (thirds, ritz_values.reshape(N_BAND, WF_DEV))).reshape(NWF, NODES)
    return residual, potential.reshape(CELLS, QUAD)
```

```python
import functools
import math

import jax
import jax.numpy as jnp
from jax import lax
from jax.experimental import pallas as pl
from jax.experimental.pallas import tpu as pltpu
from jax.sharding import PartitionSpec as P

spectrum_center = 5.0
spectrum_half = 5.5

VMEM = pl.BlockSpec(memory_space=pltpu.VMEM)
SMEM = pl.BlockSpec(memory_space=pltpu.SMEM)
bf16 = jnp.bfloat16
f32 = jnp.float32


def dot(left, right):
    return jnp.dot(left, right, preferred_element_type=f32)


def dot_rows(left, right):
    return lax.dot_general(left, right, (((1,), (1,)), ((), ())), preferred_element_type=f32)


def halves(x):
    high = x.astype(bf16)
    low = (x - high.astype(f32)).astype(bf16)
    return jnp.concatenate([high, low], axis=0)


def joined(x):
    rows = x.shape[0] // 2
    return x[:rows] + x[rows:]


def column(row):
    n = row.shape[1]
    eye = lax.broadcasted_iota(jnp.int32, (n, n), 0) == lax.broadcasted_iota(jnp.int32, (n, n), 1)
    return jnp.sum(jnp.where(eye, row, jnp.zeros_like(row)), axis=1, keepdims=True)


def one_hot(hit):
    return jnp.where(hit, 1.0, 0.0).astype(bf16)


def call(kernel, outs, *args, flops=1 << 28, smem=0):
    return pl.pallas_call(
        kernel,
        out_shape=[pltpu.VMEM(shape, dtype) for shape, dtype in outs],
        in_specs=[SMEM] * smem + [VMEM] * (len(args) - smem),
        out_specs=[VMEM] * len(outs),
        compiler_params=pltpu.CompilerParams(vmem_limit_bytes=20 << 20),
        cost_estimate=pl.CostEstimate(flops=flops, bytes_accessed=1 << 20, transcendentals=0),
    )(*args)


def pick_kernel(w_ref, face_ref, table_ref, out_ref):
    owned = w_ref.shape[1]
    count = face_ref.shape[1]
    table = one_hot(lax.broadcasted_iota(jnp.int32, (owned, count), 0) == face_ref[...])
    table_ref[...] = table
    out_ref[...] = dot(w_ref[...], table).astype(bf16)


def tables_kernel(
    w_ref, links_ref, face_ref, face_table_ref, own_ref, edge_ref, inner_ref, values_ref, state_ref
):
    owned, slots = own_ref.shape
    count = face_ref.shape[1]
    links = jnp.broadcast_to(links_ref[...], (8, slots))
    strip = 16

    def own_rows(i, carry):
        start = pl.multiple_of(i * strip, strip)
        index = lax.broadcasted_iota(jnp.int32, (strip, slots), 0) + (start + count)
        own_ref[pl.ds(start, strip), :] = one_hot(index == jnp.concatenate([links, links], axis=0))
        return carry

    lax.fori_loop(0, owned // strip, own_rows, 0, unroll=4)
    ghost_index = lax.broadcasted_iota(jnp.int32, (count, 1), 0)
    face_index = column(face_ref[...].astype(f32)).astype(jnp.int32) + count
    for part, index in enumerate((ghost_index, face_index)):
        for start in range(0, count, strip):
            rows = jnp.broadcast_to(index[start : start + strip], (strip, slots))
            edge_ref[pl.ds(part * count + start, strip), :] = one_hot(
                rows == jnp.concatenate([links, links], axis=0)
            )
    named = dot_rows(jnp.ones((8, count), bf16), face_table_ref[...])
    inner = 1.0 - named
    inner_ref[...] = inner
    w = w_ref[...]
    values_ref[...] = dot(w, own_ref[...]).astype(bf16)
    state_ref[...] = w.astype(f32) * inner[:1]


def cell_products(values, matrix_ref, out_ref):
    cells, nodes, _ = matrix_ref.shape
    pitch = values.shape[1] // cells
    out_ref[...] = jnp.zeros_like(out_ref)
    for cell in range(cells):
        start = cell * pitch
        out_ref[:, start : start + nodes] = dot(values[:, start : start + nodes], matrix_ref[cell])


def send_sums(values, matrix_ref, edge_ref, parts_ref, ghost_ref, face_ref, product_ref):
    cell_products(values, matrix_ref, product_ref)
    parts = halves(product_ref[...])
    parts_ref[...] = parts
    sums = joined(dot_rows(parts, edge_ref[...]))
    count = ghost_ref.shape[1]
    ghost_ref[...] = sums[:, :count]
    face_ref[...] = sums[:, count:]


def first_kernel(
    flags_ref, values_ref, got_ref, matrix_ref, edge_ref,
    parts_ref, ghost_ref, face_ref, state_ref, product_ref,
):
    got = got_ref[...].astype(f32)
    got = jnp.where(flags_ref[0] > 0, got, jnp.zeros_like(got))
    state_ref[...] = got
    count = got.shape[1]
    values = values_ref[...].astype(f32) + dot(got.astype(bf16), edge_ref[:count, :])
    send_sums(values.astype(bf16), matrix_ref, edge_ref, parts_ref, ghost_ref, face_ref, product_ref)


def advance(scale, applied, state, before):
    new = (applied - spectrum_center * state) * scale
    return new if before is None else new - before


def edge_step(scale, flags_ref, got_ghost, got_face, sum_ghost, sum_face, ghost, face, before):
    keep_ghost, keep_face = flags_ref[0] > 0, flags_ref[1] > 0
    arrived = got_face[...]
    applied_face = sum_face[...] + jnp.where(keep_face, arrived, jnp.zeros_like(arrived))
    new_face = advance(scale, applied_face, face[...], before and before[1][...])
    new_ghost = advance(
        scale, sum_ghost[...] + got_ghost[...], ghost[...], before and before[0][...]
    )
    new_ghost = jnp.where(keep_ghost, new_ghost, jnp.zeros_like(new_ghost))
    return new_ghost, new_face


def next_values(new_ghost, new_face, values_ref, edge_ref):
    edge = jnp.concatenate([new_ghost.astype(bf16), new_face.astype(bf16)], axis=1)
    return (values_ref[...].astype(f32) + dot(edge, edge_ref[...])).astype(bf16)


def edge_kernel(scale, with_before, flags_ref, got_ghost, got_face, sum_ghost, sum_face, ghost, face, *rest):
    before, rest = (rest[:2], rest[2:]) if with_before else (None, rest)
    values_ref, matrix_ref, edge_ref, parts_ref, out_ghost, out_face, new_ghost, new_face, product_ref = rest
    ghost_value, face_value = edge_step(
        scale, flags_ref, got_ghost, got_face, sum_ghost, sum_face, ghost, face, before
    )
    new_ghost[...] = ghost_value
    new_face[...] = face_value
    values = next_values(ghost_value, face_value, values_ref, edge_ref)
    send_sums(values, matrix_ref, edge_ref, parts_ref, out_ghost, out_face, product_ref)


def inner_kernel(scale, with_before, parts_ref, state_ref, *rest):
    before = rest[0][...] if with_before else None
    own_ref, inner_ref, new_ref, values_ref = rest[1:] if with_before else rest
    applied = joined(dot_rows(parts_ref[...], own_ref[...]))
    new = advance(scale, applied, state_ref[...], before) * inner_ref[:1]
    new_ref[...] = new
    values_ref[...] = dot(new.astype(bf16), own_ref[...]).astype(bf16)


def density_kernel(
    flags_ref, got_ghost, got_face, sum_ghost, sum_face, ghost, face, before_ghost, before_face,
    values_ref, edge_ref, basis_ref, occupancy_ref,
    new_face, final_ref, at_ref, band_ref, *, scale, cells,
):
    ghost_value, face_value = edge_step(
        scale, flags_ref, got_ghost, got_face, sum_ghost, sum_face, ghost, face,
        (before_ghost, before_face),
    )
    new_face[...] = face_value
    values = next_values(ghost_value, face_value, values_ref, edge_ref)
    final_ref[...] = values
    nodes = basis_ref.shape[0]
    waves, slots = values.shape
    pitch = slots // cells
    stacked = jnp.concatenate(
        [values[:, cell * pitch : (cell + 1) * pitch] for cell in range(cells)], axis=0
    )
    at = dot(stacked[:, :nodes], basis_ref[...])
    at_ref[...] = at
    weights = column(occupancy_ref[...])
    for cell in range(cells):
        block = at[cell * waves : (cell + 1) * waves]
        band_ref[cell : cell + 1, :] = jnp.sum(weights * (block * block), axis=0, keepdims=True)


def products_kernel(values_ref, matrix_ref, product_ref):
    cell_products(values_ref[...], matrix_ref, product_ref)


def cube_root(x):
    return jnp.exp(jnp.log(x) * (1.0 / 3.0))


def exchange_correlation(density):
    radius = cube_root(0.75 / math.pi / density)
    exchange_part = -cube_root(3.0 / math.pi * density)
    shifted_radius = radius + 7.8
    correlation_part = -0.44 / shifted_radius - 0.44 * radius / (
        3.0 * shifted_radius * shifted_radius
    )
    return exchange_part + correlation_part


def potential_kernel(total_ref, *rest, factor):
    more, (core_ref, quad_ref, at_ref, basis_ref, product_ref, edge_ref,
           potential_ref, parts_ref, ghost_ref, term_ref) = rest[:-10], rest[-10:]
    total = total_ref[...]
    if more:
        total = (total + more[0][...]) + (more[1][...] + more[2][...])
    potential = exchange_correlation(core_ref[...] + factor * total)
    potential_ref[...] = potential
    scaled = quad_ref[...] * potential
    cells = scaled.shape[0]
    waves, slots = product_ref.shape
    pitch = slots // cells
    nodes = basis_ref.shape[0]
    weighted = jnp.concatenate(
        [
            (at_ref[cell * waves : (cell + 1) * waves, :] * scaled[cell : cell + 1]).astype(bf16)
            for cell in range(cells)
        ],
        axis=0,
    )
    projected = dot_rows(weighted, basis_ref[...])
    term_ref[...] = product_ref[...]
    for cell in range(cells):
        start = cell * pitch
        term_ref[:, start : start + nodes] += projected[cell * waves : (cell + 1) * waves]
    parts = halves(term_ref[...])
    parts_ref[...] = parts
    count = ghost_ref.shape[1]
    ghost_ref[...] = joined(dot_rows(parts, edge_ref[:count, :]))


def residual_kernel(parts_ref, state_ref, face_ref, ritz_ref, own_ref, face_table_ref, out_ref):
    ritz = column(ritz_ref[...])
    faces = joined(dot_rows(halves(ritz * face_ref[...]), face_table_ref[...]))
    out_ref[...] = (
        joined(dot_rows(parts_ref[...], own_ref[...])) - ritz * state_ref[...] - faces
    )


def finish_kernel(flags_ref, got_ref, partial_ref, face_table_ref, out_ref):
    got = got_ref[...]
    got = jnp.where(flags_ref[1] > 0, got, jnp.zeros_like(got))
    out_ref[...] = partial_ref[...] + joined(dot_rows(halves(got), face_table_ref[...]))


def around(x, axis, distance):
    count = lax.axis_size(axis)
    return lax.ppermute(x, axis, [(i, (i + distance) % count) for i in range(count)])


def swapped(x, axis, mask):
    return lax.ppermute(x, axis, [(i, i ^ mask) for i in range(lax.axis_size(axis))])


def band_parts(x, axis):
    count = lax.axis_size(axis)
    if count & (count - 1):
        return [lax.psum(x, axis)]
    bit = 1
    if count > 1:
        x = x + swapped(x, axis, bit)
        bit = 2
    parts = [x]
    while bit < count:
        x = parts[0] if len(parts) == 1 else (parts[0] + parts[1]) + (parts[2] + parts[3])
        if 2 * bit < count:
            parts = [x] + [swapped(x, axis, mask) for mask in (bit, 2 * bit, 3 * bit)]
            bit *= 4
        else:
            parts = [x + swapped(x, axis, bit)]
            bit *= 2
    return parts


def shards(
    wavefunctions,
    cell_hamiltonian,
    connectivity,
    face_nodes,
    basis_values,
    quad_weights,
    core_density,
    occupancy,
    ritz_values,
):
    waves, owned = wavefunctions.shape
    count = face_nodes.shape[0]
    cells, nodes = connectivity.shape
    points = basis_values.shape[1]
    pitch = -(-nodes // 128) * 128
    slots = cells * pitch
    band_total = waves * lax.axis_size("band")
    domain = lax.axis_index("space")
    flags = jnp.stack([domain > 0, domain < lax.axis_size("space") - 1]).astype(jnp.int32)
    links = jnp.pad(connectivity, ((0, 0), (0, pitch - nodes)), constant_values=-1)
    links = links.reshape(1, slots)
    faces = face_nodes.reshape(1, count)

    edge_out = [((waves, count), f32)] * 2
    parts_out = ((2 * waves, slots), bf16)
    product_out = ((waves, slots), f32)
    values_out = ((waves, slots), bf16)
    state_out = ((waves, owned), f32)

    face_table, start_face = call(
        pick_kernel, [((owned, count), bf16), ((waves, count), bf16)], wavefunctions, faces
    )
    start_ghost = around(start_face, "space", 1)
    own, edge, inner, values, state = call(
        tables_kernel,
        [((owned, slots), bf16), ((2 * count, slots), bf16), ((8, owned), f32), values_out, state_out],
        wavefunctions, links, faces, face_table,
    )
    parts, sum_ghost, sum_face, ghost, _ = call(
        first_kernel,
        [parts_out, *edge_out, edge_out[0], product_out],
        flags, values, start_ghost, cell_hamiltonian, edge, smem=1,
    )
    face = start_face.astype(f32)
    before_edge, before_state = (), ()
    scale = 1.0 / spectrum_half
    for step in range(3):
        got_ghost = around(sum_face, "space", 1)
        got_face = around(sum_ghost, "space", -1)
        new_state, values = call(
            functools.partial(inner_kernel, scale, step > 0),
            [state_out, values_out],
            parts, state, *before_state, own, inner,
        )
        received = (flags, got_ghost, got_face, sum_ghost, sum_face, ghost, face, *before_edge)
        if step < 2:
            parts, sum_ghost, sum_face, new_ghost, new_face, _ = call(
                functools.partial(edge_kernel, scale, step > 0),
                [parts_out, *edge_out, *edge_out, product_out],
                *received, values, cell_hamiltonian, edge, smem=1,
            )
            before_edge, ghost, face = (ghost, face), new_ghost, new_face
        else:
            face, final, at, band = call(
                functools.partial(density_kernel, scale=scale, cells=cells),
                [edge_out[0], values_out, ((cells * waves, points), f32), ((cells, points), f32)],
                *received, values, edge, basis_values, occupancy.reshape(1, waves), smem=1,
            )
        before_state, state = (state,), new_state
        scale = 2.0 / spectrum_half
    (products,) = call(products_kernel, [product_out], final, cell_hamiltonian)
    totals = band_parts(band, "band")
    potential, parts, sum_ghost, _ = call(
        functools.partial(potential_kernel, factor=2.0 / band_total),
        [((cells, points), f32), parts_out, edge_out[0], product_out],
        *totals, core_density, quad_weights, at, basis_values, products, edge,
    )
    returned = around(sum_ghost, "space", -1)
    (partial,) = call(
        residual_kernel, [state_out],
        parts, state, face, ritz_values.reshape(1, waves), own, face_table,
    )
    (residual,) = call(finish_kernel, [state_out], flags, returned, partial, face_table, smem=1)
    return (residual, potential)


def solution(mesh):
    in_specs = (
        P("band", "space"),
        P("space", None, None),
        P("space", None),
        P("space"),
        P(),
        P("space", None),
        P("space", None),
        P("band"),
        P("band"),
    )
    out_specs = (P("band", "space"), P("space", None))
    return jax.shard_map(shards, mesh=mesh, in_specs=in_specs, out_specs=out_specs, check_vma=False)
```

```python
import functools
import math

import jax
import jax.numpy as jnp
from jax import lax
from jax.experimental import pallas as pl
from jax.experimental.pallas import tpu as pltpu
from jax.sharding import PartitionSpec as P

spectrum_center = 5.0
spectrum_half = 5.5

VMEM = pl.BlockSpec(memory_space=pltpu.VMEM)
SMEM = pl.BlockSpec(memory_space=pltpu.SMEM)
OUTSIDE = pl.BlockSpec(memory_space=pl.ANY)
bf16 = jnp.bfloat16
f32 = jnp.float32


def dot(left, right):
    return jnp.dot(left, right, preferred_element_type=f32)


def dot_rows(left, right):
    return lax.dot_general(left, right, (((1,), (1,)), ((), ())), preferred_element_type=f32)


def halves(x):
    high = x.astype(bf16)
    low = (x - high.astype(f32)).astype(bf16)
    return jnp.concatenate([high, low], axis=0)


def joined(x):
    rows = x.shape[0] // 2
    return x[:rows] + x[rows:]


def column(row):
    n = row.shape[1]
    eye = lax.broadcasted_iota(jnp.int32, (n, n), 0) == lax.broadcasted_iota(jnp.int32, (n, n), 1)
    return jnp.sum(jnp.where(eye, row, jnp.zeros_like(row)), axis=1, keepdims=True)


def one_hot(hit):
    return jnp.where(hit, 1.0, 0.0).astype(bf16)


def call(kernel, outs, *args, flops=1 << 28, smem=0, held=0, sent=0, scratch=()):
    count = len(args) - smem - held
    kept = len(outs) - sent
    return pl.pallas_call(
        kernel,
        out_shape=[pltpu.VMEM(*out) for out in outs[:kept]]
        + [jax.ShapeDtypeStruct(*out) for out in outs[kept:]],
        in_specs=[SMEM] * smem + [OUTSIDE] * held + [VMEM] * count,
        out_specs=[VMEM] * kept + [OUTSIDE] * sent,
        scratch_shapes=list(scratch),
        compiler_params=pltpu.CompilerParams(vmem_limit_bytes=20 << 20),
        cost_estimate=pl.CostEstimate(flops=flops, bytes_accessed=1 << 20, transcendentals=0),
    )(*args)


def pick_kernel(w_in, face_in, links_in, matrix_in, w_ref, face_ref, links_ref, matrix_ref, table_ref, out_ref, sems):
    pairs = ((w_in, w_ref), (face_in, face_ref), (links_in, links_ref), (matrix_in, matrix_ref))
    copies = [
        pltpu.make_async_copy(source, target, sems.at[i]) for i, (source, target) in enumerate(pairs)
    ]
    for copy in copies:
        copy.start()
    owned = w_ref.shape[1]
    count = face_ref.shape[1]
    copies[1].wait()
    table = one_hot(lax.broadcasted_iota(jnp.int32, (owned, count), 0) == face_ref[...])
    table_ref[...] = table
    copies[0].wait()
    out_ref[...] = dot(w_ref[...], table).astype(bf16)
    copies[2].wait()
    copies[3].wait()


def short_one_hot(left, right):
    return jnp.where(left == right, jnp.ones(left.shape, bf16), jnp.zeros(left.shape, bf16))


def across(block, width):
    return jnp.concatenate([block] * (width // block.shape[1]), axis=1)


def tables_kernel(
    w_ref, face_ref, links_ref, matrix_ref, face_table_ref,
    own_ref, edge_ref, from_own_ref, from_edge_ref, padded_ref, inner_ref, values_ref, state_ref,
    row_ref, turn_ref, wide_ref,
):
    owned, slots = own_ref.shape
    count = face_ref.shape[1]
    cells, nodes = links_ref.shape
    pitch = slots // cells
    strip, lanes = 16, 128
    short = jnp.int16

    row_ref[...] = jnp.full(row_ref.shape, -1, jnp.int32)
    turn_ref[...] = jnp.full(turn_ref.shape, -1.0, f32)
    for cell in range(cells):
        line = links_ref[cell : cell + 1, :]
        row_ref[:, cell * pitch : cell * pitch + nodes] = jnp.broadcast_to(line, (strip, nodes))
        turn_ref[cell : cell + 1, :nodes] = line.astype(f32)
    links = row_ref[...].astype(short)

    def own_rows(i, carry):
        start = pl.multiple_of(i * strip, strip)
        index = lax.broadcasted_iota(jnp.int32, (strip, lanes), 0) + (start + count)
        own_ref[pl.ds(start, strip), :] = short_one_hot(across(index.astype(short), slots), links)
        return carry

    lax.fori_loop(0, owned // strip, own_rows, 0, unroll=4)
    w = w_ref[...]
    values_ref[...] = dot(w, own_ref[...]).astype(bf16)

    ghost_index = lax.broadcasted_iota(jnp.int32, (count, 1), 0)
    face_index = column(face_ref[...].astype(f32)).astype(jnp.int32) + count
    for part, index in enumerate((ghost_index, face_index)):
        for start in range(0, count, strip):
            block = jnp.broadcast_to(index[start : start + strip], (strip, lanes)).astype(short)
            edge_ref[part * count + start : part * count + start + strip, :] = short_one_hot(
                across(block, slots), links
            )

    edge_row = jnp.concatenate(
        [
            lax.broadcasted_iota(jnp.int32, (strip, count), 1),
            jnp.broadcast_to(face_ref[...], (strip, count)) + count,
        ],
        axis=1,
    ).astype(short)
    own_row = (lax.broadcasted_iota(jnp.int32, (strip, owned), 1) + count).astype(short)
    turned = jnp.transpose(turn_ref[...])
    for cell in range(cells):
        for start in range(0, pitch, strip):
            block = jnp.broadcast_to(turned[start : start + strip, cell : cell + 1], (strip, lanes))
            block = block.astype(jnp.int32).astype(short)
            rows = slice(cell * pitch + start, cell * pitch + start + strip)
            from_edge_ref[rows, :] = short_one_hot(across(block, 2 * count), edge_row)
            from_own_ref[rows, :] = short_one_hot(across(block, owned), own_row)

    wide_ref[...] = jnp.zeros_like(wide_ref)
    for cell in range(cells):
        wide_ref[cell % 2, :nodes, :nodes] = matrix_ref[cell].astype(f32)
        padded_ref[cell] = wide_ref[cell % 2].astype(bf16)

    named = dot_rows(jnp.ones((8, count), bf16), face_table_ref[...])
    inner = 1.0 - named
    inner_ref[...] = inner
    state_ref[...] = w.astype(f32) * inner[:1]


def cell_block(values, matrix_ref, cell):
    pitch = matrix_ref.shape[1]
    return dot(values[:, cell * pitch : (cell + 1) * pitch], matrix_ref[cell])


def put_parts(parts_ref, cell, pitch, block):
    parts_ref[:, cell * pitch : (cell + 1) * pitch] = halves(block)


def send_sums(values, matrix_ref, from_edge_ref, parts_ref, ghost_ref, face_ref):
    cells, pitch, _ = matrix_ref.shape
    for cell in range(cells):
        put_parts(parts_ref, cell, pitch, cell_block(values, matrix_ref, cell))
    sums = joined(dot(parts_ref[...], from_edge_ref[...]))
    count = ghost_ref.shape[1]
    ghost_ref[...] = sums[:, :count]
    face_ref[...] = sums[:, count:]


def first_kernel(
    flags_ref, values_ref, got_ref, matrix_ref, edge_ref, from_edge_ref,
    parts_ref, ghost_ref, face_ref, state_ref,
):
    got = got_ref[...].astype(f32)
    got = jnp.where(flags_ref[0] > 0, got, jnp.zeros_like(got))
    state_ref[...] = got
    count = got.shape[1]
    values = values_ref[...].astype(f32) + dot(got.astype(bf16), edge_ref[:count, :])
    send_sums(values.astype(bf16), matrix_ref, from_edge_ref, parts_ref, ghost_ref, face_ref)


def advance(scale, applied, state, before):
    new = (applied - spectrum_center * state) * scale
    return new if before is None else new - before


def edge_step(scale, flags_ref, got_ghost, got_face, sum_ghost, sum_face, ghost, face, before):
    keep_ghost, keep_face = flags_ref[0] > 0, flags_ref[1] > 0
    arrived = got_face[...]
    applied_face = sum_face[...] + jnp.where(keep_face, arrived, jnp.zeros_like(arrived))
    new_face = advance(scale, applied_face, face[...], before and before[1][...])
    new_ghost = advance(
        scale, sum_ghost[...] + got_ghost[...], ghost[...], before and before[0][...]
    )
    new_ghost = jnp.where(keep_ghost, new_ghost, jnp.zeros_like(new_ghost))
    return new_ghost, new_face


def next_values(new_ghost, new_face, values_ref, edge_ref):
    edge = jnp.concatenate([new_ghost.astype(bf16), new_face.astype(bf16)], axis=1)
    return (values_ref[...].astype(f32) + dot(edge, edge_ref[...])).astype(bf16)


def edge_kernel(scale, with_before, flags_ref, got_ghost, got_face, sum_ghost, sum_face, ghost, face, *rest):
    before, rest = (rest[:2], rest[2:]) if with_before else (None, rest)
    values_ref, matrix_ref, edge_ref, from_edge_ref, parts_ref, out_ghost, out_face, new_ghost, new_face = rest
    ghost_value, face_value = edge_step(
        scale, flags_ref, got_ghost, got_face, sum_ghost, sum_face, ghost, face, before
    )
    new_ghost[...] = ghost_value
    new_face[...] = face_value
    values = next_values(ghost_value, face_value, values_ref, edge_ref)
    send_sums(values, matrix_ref, from_edge_ref, parts_ref, out_ghost, out_face)


def inner_kernel(scale, with_before, parts_ref, state_ref, *rest):
    before = rest[0][...] if with_before else None
    own_ref, from_own_ref, inner_ref, new_ref, values_ref = rest[1:] if with_before else rest
    applied = joined(dot(parts_ref[...], from_own_ref[...]))
    new = advance(scale, applied, state_ref[...], before) * inner_ref[:1]
    new_ref[...] = new
    values_ref[...] = dot(new.astype(bf16), own_ref[...]).astype(bf16)


def density_kernel(
    flags_ref, got_ghost, got_face, sum_ghost, sum_face, ghost, face, before_ghost, before_face,
    values_ref, edge_ref, basis_ref, occupancy_ref,
    new_face, final_ref, at_ref, band_ref, *, scale, cells,
):
    ghost_value, face_value = edge_step(
        scale, flags_ref, got_ghost, got_face, sum_ghost, sum_face, ghost, face,
        (before_ghost, before_face),
    )
    new_face[...] = face_value
    values = next_values(ghost_value, face_value, values_ref, edge_ref)
    final_ref[...] = values
    nodes = basis_ref.shape[0]
    waves, slots = values.shape
    pitch = slots // cells
    stacked = jnp.concatenate(
        [values[:, cell * pitch : (cell + 1) * pitch] for cell in range(cells)], axis=0
    )
    at = dot(stacked[:, :nodes], basis_ref[...])
    at_ref[...] = at
    weights = column(occupancy_ref[...])
    for cell in range(cells):
        block = at[cell * waves : (cell + 1) * waves]
        band_ref[cell : cell + 1, :] = jnp.sum(weights * (block * block), axis=0, keepdims=True)


def products_kernel(
    values_ref, matrix_ref, basis_ref, face_ref, product_ref, wide_basis_ref, to_face_ref, wide_ref
):
    cells, pitch, _ = matrix_ref.shape
    values = values_ref[...]
    for cell in range(cells):
        product_ref[:, cell * pitch : (cell + 1) * pitch] = cell_block(values, matrix_ref, cell)
    nodes = basis_ref.shape[0]
    wide_ref[...] = jnp.zeros_like(wide_ref)
    wide_ref[:nodes, :] = basis_ref[...].astype(f32)
    wide_basis_ref[...] = wide_ref[...].astype(bf16)
    index = column(face_ref[...].astype(f32)).astype(jnp.int32)
    to_face_ref[...] = one_hot(lax.broadcasted_iota(jnp.int32, to_face_ref.shape, 1) == index)


def cube_root(x):
    return jnp.exp(jnp.log(x) * (1.0 / 3.0))


def exchange_correlation(density):
    radius = cube_root(0.75 / math.pi / density)
    exchange_part = -cube_root(3.0 / math.pi * density)
    shifted_radius = radius + 7.8
    correlation_part = -0.44 / shifted_radius - 0.44 * radius / (
        3.0 * shifted_radius * shifted_radius
    )
    return exchange_part + correlation_part


def potential_kernel(total_ref, *rest, factor):
    more, (core_ref, quad_ref, at_ref, basis_ref, product_ref, from_edge_ref,
           potential_ref, parts_ref, ghost_ref) = rest[:-9], rest[-9:]
    total = total_ref[...]
    if more:
        total = (total + more[0][...]) + (more[1][...] + more[2][...])
    potential = exchange_correlation(core_ref[...] + factor * total)
    potential_ref[...] = potential
    scaled = quad_ref[...] * potential
    cells = scaled.shape[0]
    waves, slots = product_ref.shape
    pitch = slots // cells
    weighted = jnp.concatenate(
        [
            (at_ref[cell * waves : (cell + 1) * waves, :] * scaled[cell : cell + 1]).astype(bf16)
            for cell in range(cells)
        ],
        axis=0,
    )
    projected = dot_rows(weighted, basis_ref[...])
    for cell in range(cells):
        block = product_ref[:, cell * pitch : (cell + 1) * pitch]
        put_parts(parts_ref, cell, pitch, block + projected[cell * waves : (cell + 1) * waves])
    count = ghost_ref.shape[1]
    ghost_ref[...] = joined(dot(parts_ref[...], from_edge_ref[:, :count]))


def residual_kernel(
    parts_ref, state_ref, face_ref, ritz_ref, from_own_ref, to_face_ref, potential_ref,
    out_ref, potential_out, sem,
):
    copy = pltpu.make_async_copy(potential_ref, potential_out, sem)
    copy.start()
    ritz = column(ritz_ref[...])
    faces = joined(dot(halves(ritz * face_ref[...]), to_face_ref[...]))
    out_ref[...] = joined(dot(parts_ref[...], from_own_ref[...])) - ritz * state_ref[...] - faces
    copy.wait()


def finish_kernel(flags_ref, got_ref, partial_ref, to_face_ref, out_ref, hold_ref, sem):
    got = got_ref[...]
    got = jnp.where(flags_ref[1] > 0, got, jnp.zeros_like(got))
    hold_ref[...] = partial_ref[...] + joined(dot(halves(got), to_face_ref[...]))
    copy = pltpu.make_async_copy(hold_ref, out_ref, sem)
    copy.start()
    copy.wait()


def around(x, axis, distance):
    count = lax.axis_size(axis)
    return lax.ppermute(x, axis, [(i, (i + distance) % count) for i in range(count)])


def swapped(x, axis, mask):
    return lax.ppermute(x, axis, [(i, i ^ mask) for i in range(lax.axis_size(axis))])


def band_parts(x, axis):
    count = lax.axis_size(axis)
    if count & (count - 1):
        return [lax.psum(x, axis)]
    bit = 1
    if count > 1:
        x = x + swapped(x, axis, bit)
        bit = 2
    parts = [x]
    while bit < count:
        x = parts[0] if len(parts) == 1 else (parts[0] + parts[1]) + (parts[2] + parts[3])
        if 2 * bit < count:
            parts = [x] + [swapped(x, axis, mask) for mask in (bit, 2 * bit, 3 * bit)]
            bit *= 4
        else:
            parts = [x + swapped(x, axis, bit)]
            bit *= 2
    return parts


def shards(
    wavefunctions,
    cell_hamiltonian,
    connectivity,
    face_nodes,
    basis_values,
    quad_weights,
    core_density,
    occupancy,
    ritz_values,
):
    waves, owned = wavefunctions.shape
    count = face_nodes.shape[0]
    cells, nodes = connectivity.shape
    points = basis_values.shape[1]
    pitch = -(-nodes // 128) * 128
    slots = cells * pitch
    band_total = waves * lax.axis_size("band")
    domain = lax.axis_index("space")
    flags = jnp.stack([domain > 0, domain < lax.axis_size("space") - 1]).astype(jnp.int32)
    edge_out = [((waves, count), f32)] * 2
    parts_out = ((2 * waves, slots), bf16)
    values_out = ((waves, slots), bf16)
    state_out = ((waves, owned), f32)

    w, faces, links, matrix, face_table, start_face = call(
        pick_kernel,
        [
            (wavefunctions.shape, bf16),
            ((1, count), jnp.int32),
            (connectivity.shape, jnp.int32),
            (cell_hamiltonian.shape, bf16),
            ((owned, count), bf16),
            ((waves, count), bf16),
        ],
        wavefunctions, face_nodes.reshape(1, count), connectivity, cell_hamiltonian,
        held=4, scratch=[pltpu.SemaphoreType.DMA((4,))],
    )
    start_ghost = around(start_face, "space", 1)
    own, edge, from_own, from_edge, padded, inner, values, state = call(
        tables_kernel,
        [
            ((owned, slots), bf16),
            ((2 * count, slots), bf16),
            ((slots, owned), bf16),
            ((slots, 2 * count), bf16),
            ((cells, pitch, pitch), bf16),
            ((8, owned), f32),
            values_out,
            state_out,
        ],
        w, faces, links, matrix, face_table,
        scratch=[
            pltpu.VMEM((16, slots), jnp.int32),
            pltpu.VMEM((-(-cells // 128) * 128, pitch), f32),
            pltpu.VMEM((2, pitch, pitch), f32),
        ],
    )
    parts, sum_ghost, sum_face, ghost = call(
        first_kernel,
        [parts_out, *edge_out, edge_out[0]],
        flags, values, start_ghost, padded, edge, from_edge, smem=1,
    )
    face = start_face.astype(f32)
    before_edge, before_state = (), ()
    scale = 1.0 / spectrum_half
    for step in range(3):
        got_ghost = around(sum_face, "space", 1)
        got_face = around(sum_ghost, "space", -1)
        new_state, values = call(
            functools.partial(inner_kernel, scale, step > 0),
            [state_out, values_out],
            parts, state, *before_state, own, from_own, inner,
        )
        received = (flags, got_ghost, got_face, sum_ghost, sum_face, ghost, face, *before_edge)
        if step < 2:
            parts, sum_ghost, sum_face, new_ghost, new_face = call(
                functools.partial(edge_kernel, scale, step > 0),
                [parts_out, *edge_out, *edge_out],
                *received, values, padded, edge, from_edge, smem=1,
            )
            before_edge, ghost, face = (ghost, face), new_ghost, new_face
        else:
            face, final, at, band = call(
                functools.partial(density_kernel, scale=scale, cells=cells),
                [edge_out[0], values_out, ((cells * waves, points), f32), ((cells, points), f32)],
                *received, values, edge, basis_values, occupancy.reshape(1, waves), smem=1,
            )
        before_state, state = (state,), new_state
        scale = 2.0 / spectrum_half
    products, wide_basis, to_face = call(
        products_kernel,
        [((waves, slots), f32), ((pitch, points), bf16), ((count, owned), bf16)],
        final, padded, basis_values, faces, scratch=[pltpu.VMEM((pitch, points), f32)],
    )
    totals = band_parts(band, "band")
    potential, parts, sum_ghost = call(
        functools.partial(potential_kernel, factor=2.0 / band_total),
        [((cells, points), f32), parts_out, edge_out[0]],
        *totals, core_density, quad_weights, at, wide_basis, products, from_edge,
    )
    returned = around(sum_ghost, "space", -1)
    partial, potential = call(
        residual_kernel,
        [state_out, ((cells, points), f32)],
        parts, state, face, ritz_values.reshape(1, waves), from_own, to_face, potential,
        sent=1, scratch=[pltpu.SemaphoreType.DMA],
    )
    (residual,) = call(
        finish_kernel, [state_out], flags, returned, partial, to_face,
        smem=1, sent=1, scratch=[pltpu.VMEM(*state_out), pltpu.SemaphoreType.DMA],
    )
    return (residual, potential)


def solution(mesh):
    in_specs = (
        P("band", "space"),
        P("space", None, None),
        P("space", None),
        P("space"),
        P(),
        P("space", None),
        P("space", None),
        P("band"),
        P("band"),
    )
    out_specs = (P("band", "space"), P("space", None))
    return jax.shard_map(shards, mesh=mesh, in_specs=in_specs, out_specs=out_specs, check_vma=False)
```

```python
import functools
import math

import jax
import jax.numpy as jnp
from jax import lax
from jax.experimental import pallas as pl
from jax.experimental.pallas import tpu as pltpu
from jax.sharding import PartitionSpec as P

spectrum_center = 5.0
spectrum_half = 5.5

VMEM = pl.BlockSpec(memory_space=pltpu.VMEM)
SMEM = pl.BlockSpec(memory_space=pltpu.SMEM)
OUTSIDE = pl.BlockSpec(memory_space=pltpu.HBM)
bf16 = jnp.bfloat16
f32 = jnp.float32


def dot(left, right):
    return jnp.dot(left, right, preferred_element_type=f32)


def dot_rows(left, right):
    return lax.dot_general(left, right, (((1,), (1,)), ((), ())), preferred_element_type=f32)


def halves(x):
    high = x.astype(bf16)
    low = (x - high.astype(f32)).astype(bf16)
    return jnp.concatenate([high, low], axis=0)


def joined(x):
    rows = x.shape[0] // 2
    return x[:rows] + x[rows:]


def column(row):
    n = row.shape[1]
    eye = lax.broadcasted_iota(jnp.int32, (n, n), 0) == lax.broadcasted_iota(jnp.int32, (n, n), 1)
    return jnp.sum(jnp.where(eye, row, jnp.zeros_like(row)), axis=1, keepdims=True)


def one_hot(hit):
    return jnp.where(hit, 1.0, 0.0).astype(bf16)


def call(kernel, outs, *args, flops=1 << 28, smem=0, held=0, sent=0, scratch=(), room=20):
    count = len(args) - smem - held
    kept = len(outs) - sent
    return pl.pallas_call(
        kernel,
        out_shape=[pltpu.VMEM(*out) for out in outs[:kept]]
        + [jax.ShapeDtypeStruct(*out) for out in outs[kept:]],
        in_specs=[SMEM] * smem + [OUTSIDE] * held + [VMEM] * count,
        out_specs=[VMEM] * kept + [OUTSIDE] * sent,
        scratch_shapes=list(scratch),
        compiler_params=pltpu.CompilerParams(vmem_limit_bytes=room << 20),
        cost_estimate=pl.CostEstimate(flops=flops, bytes_accessed=1 << 20, transcendentals=0),
    )(*args)


def pick_kernel(w_in, face_in, links_in, matrix_in, w_ref, face_ref, links_ref, matrix_ref, table_ref, out_ref, sems):
    pairs = ((w_in, w_ref), (face_in, face_ref), (links_in, links_ref), (matrix_in, matrix_ref))
    copies = [
        pltpu.make_async_copy(source, target, sems.at[i]) for i, (source, target) in enumerate(pairs)
    ]
    for copy in copies:
        copy.start()
    owned = w_ref.shape[1]
    count = face_ref.shape[1]
    copies[1].wait()
    table = one_hot(lax.broadcasted_iota(jnp.int32, (owned, count), 0) == face_ref[...])
    table_ref[...] = table
    copies[0].wait()
    out_ref[...] = dot(w_ref[...], table).astype(bf16)
    copies[2].wait()
    copies[3].wait()


def short_one_hot(left, right):
    return jnp.where(left == right, jnp.ones(left.shape, bf16), jnp.zeros(left.shape, bf16))


def across(block, width):
    return jnp.concatenate([block] * (width // block.shape[1]), axis=1)


def tables_kernel(
    w_ref, face_ref, links_ref, matrix_ref, face_table_ref,
    own_ref, edge_ref, from_own_ref, from_edge_ref, padded_ref, inner_ref, values_ref, state_ref,
    row_ref, turn_ref, wide_ref,
):
    owned, slots = own_ref.shape
    count = face_ref.shape[1]
    cells, nodes = links_ref.shape
    pitch = slots // cells
    strip, lanes = 16, 128
    short = jnp.int16

    row_ref[...] = jnp.full(row_ref.shape, -1, jnp.int32)
    turn_ref[...] = jnp.full(turn_ref.shape, -1.0, f32)
    for cell in range(cells):
        line = links_ref[cell : cell + 1, :]
        row_ref[:, cell * pitch : cell * pitch + nodes] = jnp.broadcast_to(line, (strip, nodes))
        turn_ref[cell : cell + 1, :nodes] = line.astype(f32)
    links = row_ref[...].astype(short)

    def own_rows(i, carry):
        start = pl.multiple_of(i * strip, strip)
        index = lax.broadcasted_iota(jnp.int32, (strip, lanes), 0) + (start + count)
        own_ref[pl.ds(start, strip), :] = short_one_hot(across(index.astype(short), slots), links)
        return carry

    lax.fori_loop(0, owned // strip, own_rows, 0, unroll=4)
    w = w_ref[...]
    values_ref[...] = dot(w, own_ref[...]).astype(bf16)

    ghost_index = lax.broadcasted_iota(jnp.int32, (count, 1), 0)
    face_index = column(face_ref[...].astype(f32)).astype(jnp.int32) + count
    for part, index in enumerate((ghost_index, face_index)):
        for start in range(0, count, strip):
            block = jnp.broadcast_to(index[start : start + strip], (strip, lanes)).astype(short)
            edge_ref[part * count + start : part * count + start + strip, :] = short_one_hot(
                across(block, slots), links
            )

    edge_row = jnp.concatenate(
        [
            lax.broadcasted_iota(jnp.int32, (strip, count), 1),
            jnp.broadcast_to(face_ref[...], (strip, count)) + count,
        ],
        axis=1,
    ).astype(short)
    own_row = (lax.broadcasted_iota(jnp.int32, (strip, owned), 1) + count).astype(short)
    turned = jnp.transpose(turn_ref[...])
    for cell in range(cells):
        for start in range(0, pitch, strip):
            block = jnp.broadcast_to(turned[start : start + strip, cell : cell + 1], (strip, lanes))
            block = block.astype(jnp.int32).astype(short)
            rows = slice(cell * pitch + start, cell * pitch + start + strip)
            from_edge_ref[rows, :] = short_one_hot(across(block, 2 * count), edge_row)
            from_own_ref[rows, :] = short_one_hot(across(block, owned), own_row)

    wide_ref[...] = jnp.zeros_like(wide_ref)
    for cell in range(cells):
        wide_ref[cell % 2, :nodes, :nodes] = matrix_ref[cell].astype(f32)
        padded_ref[cell] = wide_ref[cell % 2].astype(bf16)

    named = dot_rows(jnp.ones((8, count), bf16), face_table_ref[...])
    inner = 1.0 - named
    inner_ref[...] = inner
    state_ref[...] = w.astype(f32) * inner[:1]


def cell_block(values, matrix_ref, cell):
    pitch = matrix_ref.shape[1]
    return dot(values[:, cell * pitch : (cell + 1) * pitch], matrix_ref[cell])


def put_parts(parts_ref, cell, pitch, block):
    parts_ref[:, cell * pitch : (cell + 1) * pitch] = halves(block)


def chosen(flags_ref, first, second):
    even = flags_ref[2] > 0
    return jnp.where(even, second, first), jnp.where(even, first, second)


def send_sums(flags_ref, values, matrix_ref, from_edge_ref, parts_ref, first_ref, second_ref):
    cells, pitch, _ = matrix_ref.shape
    for cell in range(cells):
        put_parts(parts_ref, cell, pitch, cell_block(values, matrix_ref, cell))
    sums = joined(dot(parts_ref[...], from_edge_ref[...]))
    count = first_ref.shape[1]
    first_ref[...], second_ref[...] = chosen(flags_ref, sums[:, :count], sums[:, count:])


def first_kernel(
    flags_ref, values_ref, got_first, got_second, matrix_ref, edge_ref, from_edge_ref,
    parts_ref, first_ref, second_ref, state_ref,
):
    got, _ = chosen(flags_ref, got_first[...].astype(f32), got_second[...].astype(f32))
    got = jnp.where(flags_ref[0] > 0, got, jnp.zeros_like(got))
    state_ref[...] = got
    count = got.shape[1]
    values = values_ref[...].astype(f32) + dot(got.astype(bf16), edge_ref[:count, :])
    send_sums(
        flags_ref, values.astype(bf16), matrix_ref, from_edge_ref, parts_ref, first_ref, second_ref
    )


def advance(scale, applied, state, before):
    new = (applied - spectrum_center * state) * scale
    return new if before is None else new - before


def edge_step(scale, flags_ref, got_first, got_second, sum_first, sum_second, ghost, face, before):
    keep_ghost, keep_face = flags_ref[0] > 0, flags_ref[1] > 0
    got_ghost, got_face = chosen(flags_ref, got_first[...], got_second[...])
    sum_ghost, sum_face = chosen(flags_ref, sum_first[...], sum_second[...])
    applied_face = sum_face + jnp.where(keep_face, got_face, jnp.zeros_like(got_face))
    new_face = advance(scale, applied_face, face[...], before and before[1][...])
    new_ghost = advance(scale, sum_ghost + got_ghost, ghost[...], before and before[0][...])
    new_ghost = jnp.where(keep_ghost, new_ghost, jnp.zeros_like(new_ghost))
    return new_ghost, new_face


def next_values(new_ghost, new_face, values_ref, edge_ref):
    edge = jnp.concatenate([new_ghost.astype(bf16), new_face.astype(bf16)], axis=1)
    return (values_ref[...].astype(f32) + dot(edge, edge_ref[...])).astype(bf16)


def edge_kernel(scale, with_before, flags_ref, got_first, got_second, sum_first, sum_second, ghost, face, *rest):
    before, rest = (rest[:2], rest[2:]) if with_before else (None, rest)
    values_ref, matrix_ref, edge_ref, from_edge_ref, parts_ref, out_first, out_second, new_ghost, new_face = rest
    ghost_value, face_value = edge_step(
        scale, flags_ref, got_first, got_second, sum_first, sum_second, ghost, face, before
    )
    new_ghost[...] = ghost_value
    new_face[...] = face_value
    values = next_values(ghost_value, face_value, values_ref, edge_ref)
    send_sums(flags_ref, values, matrix_ref, from_edge_ref, parts_ref, out_first, out_second)


def inner_kernel(scale, with_before, parts_ref, state_ref, *rest):
    before = rest[0][...] if with_before else None
    own_ref, from_own_ref, inner_ref, new_ref, values_ref = rest[1:] if with_before else rest
    applied = joined(dot(parts_ref[...], from_own_ref[...]))
    new = advance(scale, applied, state_ref[...], before) * inner_ref[:1]
    new_ref[...] = new
    values_ref[...] = dot(new.astype(bf16), own_ref[...]).astype(bf16)


def density_kernel(
    flags_ref, got_first, got_second, sum_first, sum_second, ghost, face, before_ghost, before_face,
    values_ref, edge_ref, basis_ref, occupancy_ref,
    new_face, final_ref, at_ref, band_ref, *, scale, cells,
):
    ghost_value, face_value = edge_step(
        scale, flags_ref, got_first, got_second, sum_first, sum_second, ghost, face,
        (before_ghost, before_face),
    )
    new_face[...] = face_value
    values = next_values(ghost_value, face_value, values_ref, edge_ref)
    final_ref[...] = values
    nodes = basis_ref.shape[0]
    waves, slots = values.shape
    pitch = slots // cells
    stacked = jnp.concatenate(
        [values[:, cell * pitch : (cell + 1) * pitch] for cell in range(cells)], axis=0
    )
    at = dot(stacked[:, :nodes], basis_ref[...])
    at_ref[...] = at
    weights = column(occupancy_ref[...])
    for cell in range(cells):
        block = at[cell * waves : (cell + 1) * waves]
        band_ref[cell : cell + 1, :] = jnp.sum(weights * (block * block), axis=0, keepdims=True)


def products_kernel(
    values_ref, matrix_ref, basis_ref, face_ref, product_ref, wide_basis_ref, to_face_ref, wide_ref
):
    cells, pitch, _ = matrix_ref.shape
    values = values_ref[...]
    for cell in range(cells):
        product_ref[:, cell * pitch : (cell + 1) * pitch] = cell_block(values, matrix_ref, cell)
    nodes = basis_ref.shape[0]
    wide_ref[...] = jnp.zeros_like(wide_ref)
    wide_ref[:nodes, :] = basis_ref[...].astype(f32)
    wide_basis_ref[...] = wide_ref[...].astype(bf16)
    index = column(face_ref[...].astype(f32)).astype(jnp.int32)
    to_face_ref[...] = one_hot(lax.broadcasted_iota(jnp.int32, to_face_ref.shape, 1) == index)


def cube_root(x):
    return jnp.exp(jnp.log(x) * (1.0 / 3.0))


def exchange_correlation(density):
    radius = cube_root(0.75 / math.pi / density)
    exchange_part = -cube_root(3.0 / math.pi * density)
    shifted_radius = radius + 7.8
    correlation_part = -0.44 / shifted_radius - 0.44 * radius / (
        3.0 * shifted_radius * shifted_radius
    )
    return exchange_part + correlation_part


def potential_kernel(total_ref, *rest, factor):
    more, (core_ref, quad_ref, at_ref, basis_ref, product_ref, from_edge_ref,
           potential_ref, parts_ref, ghost_ref) = rest[:-9], rest[-9:]
    total = total_ref[...]
    if more:
        total = (total + more[0][...]) + (more[1][...] + more[2][...])
    potential = exchange_correlation(core_ref[...] + factor * total)
    potential_ref[...] = potential
    scaled = quad_ref[...] * potential
    cells = scaled.shape[0]
    waves, slots = product_ref.shape
    pitch = slots // cells
    weighted = jnp.concatenate(
        [
            (at_ref[cell * waves : (cell + 1) * waves, :] * scaled[cell : cell + 1]).astype(bf16)
            for cell in range(cells)
        ],
        axis=0,
    )
    projected = dot_rows(weighted, basis_ref[...])
    for cell in range(cells):
        block = product_ref[:, cell * pitch : (cell + 1) * pitch]
        put_parts(parts_ref, cell, pitch, block + projected[cell * waves : (cell + 1) * waves])
    count = ghost_ref.shape[1]
    ghost_ref[...] = joined(dot(parts_ref[...], from_edge_ref[:, :count]))


def residual_kernel(
    parts_ref, state_ref, face_ref, ritz_ref, from_own_ref, to_face_ref, potential_ref,
    out_ref, potential_out, sem,
):
    copy = pltpu.make_async_copy(potential_ref, potential_out, sem)
    copy.start()
    ritz = column(ritz_ref[...])
    faces = joined(dot(halves(ritz * face_ref[...]), to_face_ref[...]))
    out_ref[...] = joined(dot(parts_ref[...], from_own_ref[...])) - ritz * state_ref[...] - faces
    copy.wait()


def finish_kernel(flags_ref, got_first, got_second, partial_ref, to_face_ref, out_ref, hold_ref, sem):
    _, got = chosen(flags_ref, got_first[...], got_second[...])
    got = jnp.where(flags_ref[1] > 0, got, jnp.zeros_like(got))
    hold_ref[...] = partial_ref[...] + joined(dot(halves(got), to_face_ref[...]))
    copy = pltpu.make_async_copy(hold_ref, out_ref, sem)
    copy.start()
    copy.wait()


def paired(x, parity):
    domains, bands = lax.axis_size("space"), lax.axis_size("band")
    route = []
    for domain in range(domains):
        other = domain + 1 if domain % 2 == parity else domain - 1
        for band in range(bands):
            target = (other, band) if 0 <= other < domains else (domain, band ^ 1 if bands % 2 == 0 else band)
            route.append((domain * bands + band, target[0] * bands + target[1]))
    return lax.ppermute(x, ("space", "band"), route)


def exchanged(first, second):
    return paired(first, 0), paired(second, 1)


def swapped(x, axis, mask):
    return lax.ppermute(x, axis, [(i, i ^ mask) for i in range(lax.axis_size(axis))])


def band_parts(x, axis):
    count = lax.axis_size(axis)
    if count & (count - 1):
        return [lax.psum(x, axis)]
    bit = 1
    if count > 1:
        x = x + swapped(x, axis, bit)
        bit = 2
    parts = [x]
    while bit < count:
        x = parts[0] if len(parts) == 1 else (parts[0] + parts[1]) + (parts[2] + parts[3])
        if 2 * bit < count:
            parts = [x] + [swapped(x, axis, mask ^ 1) for mask in (bit, 2 * bit, 3 * bit)]
            bit *= 4
        else:
            parts = [x + swapped(x, axis, bit ^ 1)]
            bit *= 2
    return parts


def shards(
    wavefunctions,
    cell_hamiltonian,
    connectivity,
    face_nodes,
    basis_values,
    quad_weights,
    core_density,
    occupancy,
    ritz_values,
):
    waves, owned = wavefunctions.shape
    count = face_nodes.shape[0]
    cells, nodes = connectivity.shape
    points = basis_values.shape[1]
    pitch = -(-nodes // 128) * 128
    slots = cells * pitch
    band_total = waves * lax.axis_size("band")
    domain = lax.axis_index("space")
    flags = jnp.stack(
        [domain > 0, domain < lax.axis_size("space") - 1, domain % 2 == 0]
    ).astype(jnp.int32)
    edge_out = [((waves, count), f32)] * 2
    parts_out = ((2 * waves, slots), bf16)
    values_out = ((waves, slots), bf16)
    state_out = ((waves, owned), f32)

    w, faces, links, matrix, face_table, start_face = call(
        pick_kernel,
        [
            (wavefunctions.shape, bf16),
            ((1, count), jnp.int32),
            (connectivity.shape, jnp.int32),
            (cell_hamiltonian.shape, bf16),
            ((owned, count), bf16),
            ((waves, count), bf16),
        ],
        wavefunctions, face_nodes.reshape(1, count), connectivity, cell_hamiltonian,
        held=4, scratch=[pltpu.SemaphoreType.DMA((4,))], room=56,
    )
    start_pair = exchanged(start_face, start_face)
    own, edge, from_own, from_edge, padded, inner, values, state = call(
        tables_kernel,
        [
            ((owned, slots), bf16),
            ((2 * count, slots), bf16),
            ((slots, owned), bf16),
            ((slots, 2 * count), bf16),
            ((cells, pitch, pitch), bf16),
            ((8, owned), f32),
            values_out,
            state_out,
        ],
        w, faces, links, matrix, face_table,
        scratch=[
            pltpu.VMEM((16, slots), jnp.int32),
            pltpu.VMEM((-(-cells // 128) * 128, pitch), f32),
            pltpu.VMEM((2, pitch, pitch), f32),
        ],
    )
    parts, *sums, ghost = call(
        first_kernel,
        [parts_out, *edge_out, edge_out[0]],
        flags, values, *start_pair, padded, edge, from_edge, smem=1,
    )
    face = start_face.astype(f32)
    before_edge, before_state = (), ()
    scale = 1.0 / spectrum_half
    for step in range(3):
        got = exchanged(*sums)
        new_state, values = call(
            functools.partial(inner_kernel, scale, step > 0),
            [state_out, values_out],
            parts, state, *before_state, own, from_own, inner,
        )
        received = (flags, *got, *sums, ghost, face, *before_edge)
        if step < 2:
            parts, *sums, new_ghost, new_face = call(
                functools.partial(edge_kernel, scale, step > 0),
                [parts_out, *edge_out, *edge_out],
                *received, values, padded, edge, from_edge, smem=1,
            )
            before_edge, ghost, face = (ghost, face), new_ghost, new_face
        else:
            face, final, at, band = call(
                functools.partial(density_kernel, scale=scale, cells=cells),
                [edge_out[0], values_out, ((cells * waves, points), f32), ((cells, points), f32)],
                *received, values, edge, basis_values, occupancy.reshape(1, waves), smem=1,
            )
        before_state, state = (state,), new_state
        scale = 2.0 / spectrum_half
    products, wide_basis, to_face = call(
        products_kernel,
        [((waves, slots), f32), ((pitch, points), bf16), ((count, owned), bf16)],
        final, padded, basis_values, faces, scratch=[pltpu.VMEM((pitch, points), f32)],
    )
    totals = band_parts(band, "band")
    potential, parts, sum_ghost = call(
        functools.partial(potential_kernel, factor=2.0 / band_total),
        [((cells, points), f32), parts_out, edge_out[0]],
        *totals, core_density, quad_weights, at, wide_basis, products, from_edge,
    )
    returned = exchanged(sum_ghost, sum_ghost)
    partial, potential = call(
        residual_kernel,
        [state_out, ((cells, points), f32)],
        parts, state, face, ritz_values.reshape(1, waves), from_own, to_face, potential,
        sent=1, scratch=[pltpu.SemaphoreType.DMA],
    )
    (residual,) = call(
        finish_kernel, [state_out], flags, *returned, partial, to_face,
        smem=1, sent=1, scratch=[pltpu.VMEM(*state_out), pltpu.SemaphoreType.DMA],
    )
    return (residual, potential)


def solution(mesh):
    in_specs = (
        P("band", "space"),
        P("space", None, None),
        P("space", None),
        P("space"),
        P(),
        P("space", None),
        P("space", None),
        P("band"),
        P("band"),
    )
    out_specs = (P("band", "space"), P("space", None))
    return jax.shard_map(shards, mesh=mesh, in_specs=in_specs, out_specs=out_specs, check_vma=False)
```

```python
import functools
import math

import jax
import jax.numpy as jnp
from jax import lax
from jax.experimental import pallas as pl
from jax.experimental.pallas import tpu as pltpu
from jax.sharding import PartitionSpec as P

spectrum_center = 5.0
spectrum_half = 5.5

VMEM = pl.BlockSpec(memory_space=pltpu.VMEM)
SMEM = pl.BlockSpec(memory_space=pltpu.SMEM)
OUTSIDE = pl.BlockSpec(memory_space=pltpu.HBM)
bf16 = jnp.bfloat16
f32 = jnp.float32


def dot(left, right):
    return jnp.dot(left, right, preferred_element_type=f32)


def dot_rows(left, right):
    return lax.dot_general(left, right, (((1,), (1,)), ((), ())), preferred_element_type=f32)


def halves(x):
    high = x.astype(bf16)
    low = (x - high.astype(f32)).astype(bf16)
    return jnp.concatenate([high, low], axis=0)


def joined(x):
    rows = x.shape[0] // 2
    return x[:rows] + x[rows:]


def column(row):
    n = row.shape[1]
    eye = lax.broadcasted_iota(jnp.int32, (n, n), 0) == lax.broadcasted_iota(jnp.int32, (n, n), 1)
    return jnp.sum(jnp.where(eye, row, jnp.zeros_like(row)), axis=1, keepdims=True)


def one_hot(hit):
    return jnp.where(hit, 1.0, 0.0).astype(bf16)


def call(kernel, outs, *args, flops=1 << 28, smem=0, held=0, sent=0, scratch=(), room=20):
    count = len(args) - smem - held
    kept = len(outs) - sent
    return pl.pallas_call(
        kernel,
        out_shape=[pltpu.VMEM(*out) for out in outs[:kept]]
        + [jax.ShapeDtypeStruct(*out) for out in outs[kept:]],
        in_specs=[SMEM] * smem + [OUTSIDE] * held + [VMEM] * count,
        out_specs=[VMEM] * kept + [OUTSIDE] * sent,
        scratch_shapes=list(scratch),
        compiler_params=pltpu.CompilerParams(vmem_limit_bytes=room << 20),
        cost_estimate=pl.CostEstimate(flops=flops, bytes_accessed=1 << 20, transcendentals=0),
    )(*args)


LANES = 128
ROWS = 16
ALONG = lax.GatherDimensionNumbers(
    offset_dims=(),
    collapsed_slice_dims=(1,),
    start_index_map=(1,),
    operand_batching_dims=(0,),
    start_indices_batching_dims=(0,),
)


def along(block, lane):
    return lax.gather(
        block, lane[..., None], ALONG, slice_sizes=(1, 1),
        mode=lax.GatherScatterMode.PROMISE_IN_BOUNDS,
    )


def gathered(source, lane, block, start=None):
    out = jnp.zeros(lane.shape, source.dtype) if start is None else start
    for number in range(source.shape[1] // LANES):
        part = along(source[:, number * LANES : (number + 1) * LANES], lane)
        out = jnp.where(block == number, part, out)
    return out


def gather_columns(source, lane_ref, block_ref, start, put):
    rows = lane_ref.shape[0]
    for column_start in range(0, lane_ref.shape[1], LANES):
        columns = slice(column_start, column_start + LANES)
        lane, block = lane_ref[:, columns], block_ref[:, columns]
        for row in range(0, source.shape[0], rows):
            begin = None if start is None else start[row : row + rows, columns]
            put(slice(row, row + rows), columns, gathered(source[row : row + rows], lane, block, begin))


def split_index(index, dtype):
    return (index & (LANES - 1)).astype(dtype), (index >> 7).astype(dtype)


def pick_kernel(w_in, face_in, links_in, w_ref, face_ref, links_ref, out_ref, sems):
    pairs = ((w_in, w_ref), (face_in, face_ref), (links_in, links_ref))
    copies = [
        pltpu.make_async_copy(source, target, sems.at[i]) for i, (source, target) in enumerate(pairs)
    ]
    for copy in copies:
        copy.start()
    for copy in copies:
        copy.wait()
    count = face_ref.shape[1]
    w = w_ref[...]
    for start in range(0, count, LANES):
        index = jnp.broadcast_to(face_ref[:, start : start + LANES], (ROWS, LANES))
        lane, block = split_index(index, jnp.int16)
        for row in range(0, w.shape[0], ROWS):
            out_ref[row : row + ROWS, start : start + LANES] = gathered(w[row : row + ROWS], lane, block)


def short_one_hot(left, right):
    return jnp.where(left == right, jnp.ones(left.shape, bf16), jnp.zeros(left.shape, bf16))


def across(block, width):
    return jnp.concatenate([block] * (width // block.shape[1]), axis=1)


def tables_kernel(
    matrix_in, w_ref, face_ref, links_ref,
    from_own_ref, from_edge_ref, padded_ref, own_lane, own_block, edge_lane, edge_block,
    node_lane, node_block, inner_ref, values_ref, state_ref,
    row_ref, turn_ref, wide_ref, table_ref, matrix_ref, sem,
):
    copy = pltpu.make_async_copy(matrix_in, matrix_ref, sem)
    copy.start()
    slots, owned = from_own_ref.shape
    count = face_ref.shape[1]
    cells, nodes = links_ref.shape
    pitch = slots // cells
    short = jnp.int16
    half = ROWS // 2

    row_ref[...] = jnp.full(row_ref.shape, -1, jnp.int32)
    turn_ref[...] = jnp.full(turn_ref.shape, -1.0, f32)
    for cell in range(cells):
        line = links_ref[cell : cell + 1, :]
        row_ref[:, cell * pitch : cell * pitch + nodes] = jnp.broadcast_to(line, (half, nodes))
        turn_ref[cell : cell + 1, :nodes] = line.astype(f32)

    table_ref[...] = one_hot(lax.broadcasted_iota(jnp.int32, (owned, count), 0) == face_ref[...])
    order = lax.broadcasted_iota(jnp.int32, (half, count), 1)
    digits = jnp.concatenate([order >> 7, (order & (LANES - 1)) + 1], axis=0)
    sums = dot_rows(digits.astype(f32).astype(bf16), table_ref[...])
    place = sums[:half] * float(LANES) + sums[half:]
    node_lane[...], node_block[...] = split_index(place.astype(jnp.int32) - 1, jnp.int32)
    inner = jnp.where(place > 0.5, 0.0, 1.0)
    inner_ref[...] = inner

    for start in range(0, slots, LANES):
        columns = slice(start, start + LANES)
        index = row_ref[:, columns]
        lane, block = split_index(index - count, jnp.int32)
        own_lane[:, columns] = jnp.concatenate([lane, lane], axis=0).astype(short)
        own_block[:, columns] = jnp.concatenate([block, block], axis=0).astype(short)
        at_face = gathered(place, lane, block).astype(jnp.int32)
        index = jnp.where(index < count, index, jnp.where(at_face > 0, at_face + (count - 1), -1))
        lane, block = split_index(index, jnp.int32)
        edge_lane[:, columns] = jnp.concatenate([lane, lane], axis=0).astype(short)
        edge_block[:, columns] = jnp.concatenate([block, block], axis=0).astype(short)

    w = w_ref[...]
    gather_columns(w, own_lane, own_block, None, functools.partial(store, values_ref))
    state_ref[...] = w.astype(f32) * inner[:1]

    edge_row = jnp.concatenate(
        [
            lax.broadcasted_iota(jnp.int32, (ROWS, count), 1),
            jnp.broadcast_to(face_ref[...], (ROWS, count)) + count,
        ],
        axis=1,
    ).astype(short)
    own_row = (lax.broadcasted_iota(jnp.int32, (ROWS, owned), 1) + count).astype(short)
    turned = jnp.transpose(turn_ref[...])
    for cell in range(cells):
        for start in range(0, pitch, ROWS):
            block = jnp.broadcast_to(turned[start : start + ROWS, cell : cell + 1], (ROWS, LANES))
            block = block.astype(jnp.int32).astype(short)
            rows = slice(cell * pitch + start, cell * pitch + start + ROWS)
            from_edge_ref[rows, :] = short_one_hot(across(block, 2 * count), edge_row)
            from_own_ref[rows, :] = short_one_hot(across(block, owned), own_row)

    wide_ref[...] = jnp.zeros_like(wide_ref)
    copy.wait()
    for cell in range(cells):
        wide_ref[cell % 2, :nodes, :nodes] = matrix_ref[cell].astype(f32)
        padded_ref[cell] = wide_ref[cell % 2].astype(bf16)


def store(ref, rows, columns, values):
    ref[rows, columns] = values


def cell_block(values, matrix_ref, cell):
    pitch = matrix_ref.shape[1]
    return dot(values[:, cell * pitch : (cell + 1) * pitch], matrix_ref[cell])


def put_parts(parts_ref, cell, pitch, block):
    parts_ref[:, cell * pitch : (cell + 1) * pitch] = halves(block)


def chosen(flags_ref, first, second):
    even = flags_ref[2] > 0
    return jnp.where(even, second, first), jnp.where(even, first, second)


def send_sums(flags_ref, values, matrix_ref, from_edge_ref, parts_ref, first_ref, second_ref):
    cells, pitch, _ = matrix_ref.shape
    for cell in range(cells):
        put_parts(parts_ref, cell, pitch, cell_block(values, matrix_ref, cell))
    sums = joined(dot(parts_ref[...], from_edge_ref[...]))
    count = first_ref.shape[1]
    first_ref[...], second_ref[...] = chosen(flags_ref, sums[:, :count], sums[:, count:])


def first_kernel(
    flags_ref, inner_values_ref, got_first, got_second, edge_lane, edge_block, matrix_ref, from_edge_ref,
    parts_ref, first_ref, second_ref, state_ref, values_ref,
):
    got, _ = chosen(flags_ref, got_first[...].astype(f32), got_second[...].astype(f32))
    got = jnp.where(flags_ref[0] > 0, got, jnp.zeros_like(got))
    state_ref[...] = got
    gather_columns(
        got.astype(bf16), edge_lane, edge_block, inner_values_ref, functools.partial(store, values_ref)
    )
    send_sums(flags_ref, values_ref[...], matrix_ref, from_edge_ref, parts_ref, first_ref, second_ref)


def advance(scale, applied, state, before):
    new = (applied - spectrum_center * state) * scale
    return new if before is None else new - before


def edge_step(scale, flags_ref, got_first, got_second, sum_first, sum_second, ghost, face, before):
    keep_ghost, keep_face = flags_ref[0] > 0, flags_ref[1] > 0
    got_ghost, got_face = chosen(flags_ref, got_first[...], got_second[...])
    sum_ghost, sum_face = chosen(flags_ref, sum_first[...], sum_second[...])
    applied_face = sum_face + jnp.where(keep_face, got_face, jnp.zeros_like(got_face))
    new_face = advance(scale, applied_face, face[...], before and before[1][...])
    new_ghost = advance(scale, sum_ghost + got_ghost, ghost[...], before and before[0][...])
    new_ghost = jnp.where(keep_ghost, new_ghost, jnp.zeros_like(new_ghost))
    return new_ghost, new_face


def next_values(new_ghost, new_face, inner_values_ref, edge_lane, edge_block, values_ref):
    edge = jnp.concatenate([new_ghost.astype(bf16), new_face.astype(bf16)], axis=1)
    gather_columns(
        edge, edge_lane, edge_block, inner_values_ref, functools.partial(store, values_ref)
    )


def edge_kernel(scale, with_before, flags_ref, got_first, got_second, sum_first, sum_second, ghost, face, *rest):
    before, rest = (rest[:2], rest[2:]) if with_before else (None, rest)
    inner_values_ref, edge_lane, edge_block, matrix_ref, from_edge_ref, *outs = rest
    parts_ref, out_first, out_second, new_ghost, new_face, values_ref = outs
    ghost_value, face_value = edge_step(
        scale, flags_ref, got_first, got_second, sum_first, sum_second, ghost, face, before
    )
    new_ghost[...] = ghost_value
    new_face[...] = face_value
    next_values(ghost_value, face_value, inner_values_ref, edge_lane, edge_block, values_ref)
    send_sums(flags_ref, values_ref[...], matrix_ref, from_edge_ref, parts_ref, out_first, out_second)


def inner_kernel(scale, with_before, parts_ref, state_ref, *rest):
    before = rest[0][...] if with_before else None
    own_lane, own_block, from_own_ref, inner_ref, new_ref, values_ref = (
        rest[1:] if with_before else rest
    )
    applied = joined(dot(parts_ref[...], from_own_ref[...]))
    new = advance(scale, applied, state_ref[...], before) * inner_ref[:1]
    new_ref[...] = new
    gather_columns(
        new.astype(bf16), own_lane, own_block, None, functools.partial(store, values_ref)
    )


def density_kernel(
    flags_ref, got_first, got_second, sum_first, sum_second, ghost, face, before_ghost, before_face,
    inner_values_ref, edge_lane, edge_block, basis_ref, occupancy_ref,
    new_face, final_ref, at_ref, band_ref, *, scale, cells,
):
    ghost_value, face_value = edge_step(
        scale, flags_ref, got_first, got_second, sum_first, sum_second, ghost, face,
        (before_ghost, before_face),
    )
    new_face[...] = face_value
    next_values(ghost_value, face_value, inner_values_ref, edge_lane, edge_block, final_ref)
    values = final_ref[...]
    nodes = basis_ref.shape[0]
    waves, slots = values.shape
    pitch = slots // cells
    stacked = jnp.concatenate(
        [values[:, cell * pitch : (cell + 1) * pitch] for cell in range(cells)], axis=0
    )
    at = dot(stacked[:, :nodes], basis_ref[...])
    at_ref[...] = at
    weights = column(occupancy_ref[...])
    for cell in range(cells):
        block = at[cell * waves : (cell + 1) * waves]
        band_ref[cell : cell + 1, :] = jnp.sum(weights * (block * block), axis=0, keepdims=True)


def products_kernel(
    values_ref, matrix_ref, basis_ref, product_ref, wide_basis_ref, wide_ref
):
    cells, pitch, _ = matrix_ref.shape
    values = values_ref[...]
    for cell in range(cells):
        product_ref[:, cell * pitch : (cell + 1) * pitch] = cell_block(values, matrix_ref, cell)
    nodes = basis_ref.shape[0]
    wide_ref[...] = jnp.zeros_like(wide_ref)
    wide_ref[:nodes, :] = basis_ref[...].astype(f32)
    wide_basis_ref[...] = wide_ref[...].astype(bf16)


def cube_root(x):
    return jnp.exp(jnp.log(x) * (1.0 / 3.0))


def exchange_correlation(density):
    radius = cube_root(0.75 / math.pi / density)
    exchange_part = -cube_root(3.0 / math.pi * density)
    shifted_radius = radius + 7.8
    correlation_part = -0.44 / shifted_radius - 0.44 * radius / (
        3.0 * shifted_radius * shifted_radius
    )
    return exchange_part + correlation_part


def potential_kernel(total_ref, *rest, factor):
    more, (core_ref, quad_ref, at_ref, basis_ref, product_ref, from_edge_ref,
           potential_ref, parts_ref, ghost_ref) = rest[:-9], rest[-9:]
    total = total_ref[...]
    if more:
        total = (total + more[0][...]) + (more[1][...] + more[2][...])
    potential = exchange_correlation(core_ref[...] + factor * total)
    potential_ref[...] = potential
    scaled = quad_ref[...] * potential
    cells = scaled.shape[0]
    waves, slots = product_ref.shape
    pitch = slots // cells
    weighted = jnp.concatenate(
        [
            (at_ref[cell * waves : (cell + 1) * waves, :] * scaled[cell : cell + 1]).astype(bf16)
            for cell in range(cells)
        ],
        axis=0,
    )
    projected = dot_rows(weighted, basis_ref[...])
    for cell in range(cells):
        block = product_ref[:, cell * pitch : (cell + 1) * pitch]
        put_parts(parts_ref, cell, pitch, block + projected[cell * waves : (cell + 1) * waves])
    count = ghost_ref.shape[1]
    ghost_ref[...] = joined(dot(parts_ref[...], from_edge_ref[:, :count]))


def residual_kernel(
    parts_ref, state_ref, face_ref, ritz_ref, from_own_ref, potential_ref,
    out_ref, shift_ref, potential_out, sem,
):
    copy = pltpu.make_async_copy(potential_ref, potential_out, sem)
    copy.start()
    ritz = column(ritz_ref[...])
    shift_ref[...] = ritz * face_ref[...]
    out_ref[...] = joined(dot(parts_ref[...], from_own_ref[...])) - ritz * state_ref[...]
    copy.wait()


def finish_kernel(
    flags_ref, got_first, got_second, partial_ref, shift_ref, node_lane, node_block,
    out_ref, hold_ref, sem,
):
    _, got = chosen(flags_ref, got_first[...], got_second[...])
    got = jnp.where(flags_ref[1] > 0, got, jnp.zeros_like(got)) - shift_ref[...]

    def add(rows, columns, values):
        hold_ref[rows, columns] = partial_ref[rows, columns] + values

    gather_columns(got, node_lane, node_block, None, add)
    copy = pltpu.make_async_copy(hold_ref, out_ref, sem)
    copy.start()
    copy.wait()


def paired(x, parity):
    domains, bands = lax.axis_size("space"), lax.axis_size("band")
    route = []
    for domain in range(domains):
        other = domain + 1 if domain % 2 == parity else domain - 1
        for band in range(bands):
            target = (other, band) if 0 <= other < domains else (domain, band ^ 1 if bands % 2 == 0 else band)
            route.append((domain * bands + band, target[0] * bands + target[1]))
    return lax.ppermute(x, ("space", "band"), route)


def exchanged(first, second):
    return paired(first, 0), paired(second, 1)


def swapped(x, axis, mask):
    return lax.ppermute(x, axis, [(i, i ^ mask) for i in range(lax.axis_size(axis))])


def band_parts(x, axis):
    count = lax.axis_size(axis)
    if count & (count - 1):
        return [lax.psum(x, axis)]
    bit = 1
    if count > 1:
        x = x + swapped(x, axis, bit)
        bit = 2
    parts = [x]
    while bit < count:
        x = parts[0] if len(parts) == 1 else (parts[0] + parts[1]) + (parts[2] + parts[3])
        if 2 * bit < count:
            parts = [x] + [swapped(x, axis, mask ^ 1) for mask in (bit, 2 * bit, 3 * bit)]
            bit *= 4
        else:
            parts = [x + swapped(x, axis, bit ^ 1)]
            bit *= 2
    return parts


def shards(
    wavefunctions,
    cell_hamiltonian,
    connectivity,
    face_nodes,
    basis_values,
    quad_weights,
    core_density,
    occupancy,
    ritz_values,
):
    waves, owned = wavefunctions.shape
    count = face_nodes.shape[0]
    cells, nodes = connectivity.shape
    points = basis_values.shape[1]
    pitch = -(-nodes // 128) * 128
    slots = cells * pitch
    band_total = waves * lax.axis_size("band")
    domain = lax.axis_index("space")
    flags = jnp.stack(
        [domain > 0, domain < lax.axis_size("space") - 1, domain % 2 == 0]
    ).astype(jnp.int32)
    edge_out = [((waves, count), f32)] * 2
    parts_out = ((2 * waves, slots), bf16)
    values_out = ((waves, slots), bf16)
    state_out = ((waves, owned), f32)

    index_out = ((ROWS, slots), jnp.int16)
    w, faces, links, start_face = call(
        pick_kernel,
        [
            (wavefunctions.shape, bf16),
            ((1, count), jnp.int32),
            (connectivity.shape, jnp.int32),
            ((waves, count), bf16),
        ],
        wavefunctions, face_nodes.reshape(1, count), connectivity,
        held=3, scratch=[pltpu.SemaphoreType.DMA((3,))], room=56,
    )
    start_pair = exchanged(start_face, start_face)
    (
        from_own, from_edge, padded, own_lane, own_block, edge_lane, edge_block,
        node_lane, node_block, inner, values, state,
    ) = call(
        tables_kernel,
        [
            ((slots, owned), bf16),
            ((slots, 2 * count), bf16),
            ((cells, pitch, pitch), bf16),
            *[index_out] * 4,
            ((ROWS // 2, owned), jnp.int32),
            ((ROWS // 2, owned), jnp.int32),
            ((ROWS // 2, owned), f32),
            values_out,
            state_out,
        ],
        cell_hamiltonian, w, faces, links,
        held=1,
        scratch=[
            pltpu.VMEM((ROWS // 2, slots), jnp.int32),
            pltpu.VMEM((-(-cells // LANES) * LANES, pitch), f32),
            pltpu.VMEM((2, pitch, pitch), f32),
            pltpu.VMEM((owned, count), bf16),
            pltpu.VMEM(cell_hamiltonian.shape, bf16),
            pltpu.SemaphoreType.DMA,
        ],
        room=44,
    )
    parts, *sums, ghost, _ = call(
        first_kernel,
        [parts_out, *edge_out, edge_out[0], values_out],
        flags, values, *start_pair, edge_lane, edge_block, padded, from_edge, smem=1,
    )
    face = start_face.astype(f32)
    before_edge, before_state = (), ()
    scale = 1.0 / spectrum_half
    for step in range(3):
        got = exchanged(*sums)
        new_state, values = call(
            functools.partial(inner_kernel, scale, step > 0),
            [state_out, values_out],
            parts, state, *before_state, own_lane, own_block, from_own, inner,
        )
        received = (flags, *got, *sums, ghost, face, *before_edge)
        if step < 2:
            parts, *sums, new_ghost, new_face, _ = call(
                functools.partial(edge_kernel, scale, step > 0),
                [parts_out, *edge_out, *edge_out, values_out],
                *received, values, edge_lane, edge_block, padded, from_edge, smem=1,
            )
            before_edge, ghost, face = (ghost, face), new_ghost, new_face
        else:
            face, final, at, band = call(
                functools.partial(density_kernel, scale=scale, cells=cells),
                [edge_out[0], values_out, ((cells * waves, points), f32), ((cells, points), f32)],
                *received, values, edge_lane, edge_block, basis_values, occupancy.reshape(1, waves), smem=1,
            )
        before_state, state = (state,), new_state
        scale = 2.0 / spectrum_half
    products, wide_basis = call(
        products_kernel,
        [((waves, slots), f32), ((pitch, points), bf16)],
        final, padded, basis_values, scratch=[pltpu.VMEM((pitch, points), f32)],
    )
    totals = band_parts(band, "band")
    potential, parts, sum_ghost = call(
        functools.partial(potential_kernel, factor=2.0 / band_total),
        [((cells, points), f32), parts_out, edge_out[0]],
        *totals, core_density, quad_weights, at, wide_basis, products, from_edge,
    )
    returned = exchanged(sum_ghost, sum_ghost)
    partial, shift, potential = call(
        residual_kernel,
        [state_out, edge_out[0], ((cells, points), f32)],
        parts, state, face, ritz_values.reshape(1, waves), from_own, potential,
        sent=1, scratch=[pltpu.SemaphoreType.DMA],
    )
    (residual,) = call(
        finish_kernel, [state_out], flags, *returned, partial, shift, node_lane, node_block,
        smem=1, sent=1, scratch=[pltpu.VMEM(*state_out), pltpu.SemaphoreType.DMA],
    )
    return (residual, potential)


def solution(mesh):
    in_specs = (
        P("band", "space"),
        P("space", None, None),
        P("space", None),
        P("space"),
        P(),
        P("space", None),
        P("space", None),
        P("band"),
        P("band"),
    )
    out_specs = (P("band", "space"), P("space", None))
    return jax.shard_map(shards, mesh=mesh, in_specs=in_specs, out_specs=out_specs, check_vma=False)
```

```python
import functools
import math

import jax
import jax.numpy as jnp
from jax import lax
from jax.experimental import pallas as pl
from jax.experimental.pallas import tpu as pltpu
from jax.sharding import PartitionSpec as P

spectrum_center = 5.0
spectrum_half = 5.5

VMEM = pl.BlockSpec(memory_space=pltpu.VMEM)
SMEM = pl.BlockSpec(memory_space=pltpu.SMEM)
OUTSIDE = pl.BlockSpec(memory_space=pltpu.HBM)
bf16 = jnp.bfloat16
f32 = jnp.float32


def dot(left, right):
    return jnp.dot(left, right, preferred_element_type=f32)


def dot_rows(left, right):
    return lax.dot_general(left, right, (((1,), (1,)), ((), ())), preferred_element_type=f32)


def halves(x):
    high = x.astype(bf16)
    low = (x - high.astype(f32)).astype(bf16)
    return jnp.concatenate([high, low], axis=0)


def joined(x):
    rows = x.shape[0] // 2
    return x[:rows] + x[rows:]


def column(row):
    n = row.shape[1]
    eye = lax.broadcasted_iota(jnp.int32, (n, n), 0) == lax.broadcasted_iota(jnp.int32, (n, n), 1)
    return jnp.sum(jnp.where(eye, row, jnp.zeros_like(row)), axis=1, keepdims=True)


def one_hot(hit):
    return jnp.where(hit, 1.0, 0.0).astype(bf16)


def call(kernel, outs, *args, flops=1 << 28, smem=0, held=0, sent=0, scratch=(), room=20):
    count = len(args) - smem - held
    kept = len(outs) - sent
    return pl.pallas_call(
        kernel,
        out_shape=[pltpu.VMEM(*out) for out in outs[:kept]]
        + [jax.ShapeDtypeStruct(*out) for out in outs[kept:]],
        in_specs=[SMEM] * smem + [OUTSIDE] * held + [VMEM] * count,
        out_specs=[VMEM] * kept + [OUTSIDE] * sent,
        scratch_shapes=list(scratch),
        compiler_params=pltpu.CompilerParams(vmem_limit_bytes=room << 20),
        cost_estimate=pl.CostEstimate(flops=flops, bytes_accessed=1 << 20, transcendentals=0),
    )(*args)


LANES = 128
ROWS = 16
ALONG = lax.GatherDimensionNumbers(
    offset_dims=(),
    collapsed_slice_dims=(1,),
    start_index_map=(1,),
    operand_batching_dims=(0,),
    start_indices_batching_dims=(0,),
)


def along(block, lane):
    return lax.gather(
        block, lane[..., None], ALONG, slice_sizes=(1, 1),
        mode=lax.GatherScatterMode.PROMISE_IN_BOUNDS,
    )


def gathered(source, lane, block, start=None):
    out = jnp.zeros(lane.shape, source.dtype) if start is None else start
    for number in range(source.shape[1] // LANES):
        part = along(source[:, number * LANES : (number + 1) * LANES], lane)
        out = jnp.where(block == number, part, out)
    return out


def gather_columns(source, lane_ref, block_ref, start, put):
    rows = lane_ref.shape[0]
    for column_start in range(0, lane_ref.shape[1], LANES):
        columns = slice(column_start, column_start + LANES)
        lane, block = lane_ref[:, columns], block_ref[:, columns]
        for row in range(0, source.shape[0], rows):
            begin = None if start is None else start[row : row + rows, columns]
            put(slice(row, row + rows), columns, gathered(source[row : row + rows], lane, block, begin))


def split_index(index, dtype):
    return (index & (LANES - 1)).astype(dtype), (index >> 7).astype(dtype)


def pick_kernel(w_in, face_in, links_in, w_ref, face_ref, links_ref, out_ref, twin_ref, sems):
    pairs = ((w_in, w_ref), (face_in, face_ref), (links_in, links_ref))
    copies = [
        pltpu.make_async_copy(source, target, sems.at[i]) for i, (source, target) in enumerate(pairs)
    ]
    for copy in copies:
        copy.start()
    for copy in copies:
        copy.wait()
    count = face_ref.shape[1]
    w = w_ref[...]
    for start in range(0, count, LANES):
        index = jnp.broadcast_to(face_ref[:, start : start + LANES], (ROWS, LANES))
        lane, block = split_index(index, jnp.int16)
        for row in range(0, w.shape[0], ROWS):
            picked = gathered(w[row : row + ROWS], lane, block)
            out_ref[row : row + ROWS, start : start + LANES] = picked
            twin_ref[row : row + ROWS, start : start + LANES] = picked


def short_one_hot(left, right):
    return jnp.where(left == right, jnp.ones(left.shape, bf16), jnp.zeros(left.shape, bf16))


def across(block, width):
    return jnp.concatenate([block] * (width // block.shape[1]), axis=1)


def tables_kernel(
    matrix_in, w_ref, face_ref, links_ref,
    from_own_ref, from_edge_ref, padded_ref, own_lane, own_block, edge_lane, edge_block,
    node_lane, node_block, inner_ref, values_ref, state_ref,
    row_ref, turn_ref, wide_ref, table_ref, matrix_ref, sem,
):
    copy = pltpu.make_async_copy(matrix_in, matrix_ref, sem)
    copy.start()
    slots, owned = from_own_ref.shape
    count = face_ref.shape[1]
    cells, nodes = links_ref.shape
    pitch = slots // cells
    short = jnp.int16
    half = ROWS // 2

    row_ref[...] = jnp.full(row_ref.shape, -1, jnp.int32)
    turn_ref[...] = jnp.full(turn_ref.shape, -1.0, f32)
    for cell in range(cells):
        line = links_ref[cell : cell + 1, :]
        row_ref[:, cell * pitch : cell * pitch + nodes] = jnp.broadcast_to(line, (half, nodes))
        turn_ref[cell : cell + 1, :nodes] = line.astype(f32)

    table_ref[...] = one_hot(lax.broadcasted_iota(jnp.int32, (owned, count), 0) == face_ref[...])
    order = lax.broadcasted_iota(jnp.int32, (half, count), 1)
    digits = jnp.concatenate([order >> 7, (order & (LANES - 1)) + 1], axis=0)
    sums = dot_rows(digits.astype(f32).astype(bf16), table_ref[...])
    place = sums[:half] * float(LANES) + sums[half:]
    node_lane[...], node_block[...] = split_index(place.astype(jnp.int32) - 1, jnp.int32)
    inner = jnp.where(place > 0.5, 0.0, 1.0)
    inner_ref[...] = inner

    for start in range(0, slots, LANES):
        columns = slice(start, start + LANES)
        index = row_ref[:, columns]
        lane, block = split_index(index - count, jnp.int32)
        own_lane[:, columns] = jnp.concatenate([lane, lane], axis=0).astype(short)
        own_block[:, columns] = jnp.concatenate([block, block], axis=0).astype(short)
        at_face = gathered(place, lane, block).astype(jnp.int32)
        index = jnp.where(index < count, index, jnp.where(at_face > 0, at_face + (count - 1), -1))
        lane, block = split_index(index, jnp.int32)
        edge_lane[:, columns] = jnp.concatenate([lane, lane], axis=0).astype(short)
        edge_block[:, columns] = jnp.concatenate([block, block], axis=0).astype(short)

    w = w_ref[...]
    gather_columns(w, own_lane, own_block, None, functools.partial(store, values_ref))
    state_ref[...] = w.astype(f32) * inner[:1]

    edge_row = jnp.concatenate(
        [
            lax.broadcasted_iota(jnp.int32, (ROWS, count), 1),
            jnp.broadcast_to(face_ref[...], (ROWS, count)) + count,
        ],
        axis=1,
    ).astype(short)
    own_row = (lax.broadcasted_iota(jnp.int32, (ROWS, owned), 1) + count).astype(short)
    turned = jnp.transpose(turn_ref[...])
    for cell in range(cells):
        for start in range(0, pitch, ROWS):
            block = jnp.broadcast_to(turned[start : start + ROWS, cell : cell + 1], (ROWS, LANES))
            block = block.astype(jnp.int32).astype(short)
            rows = slice(cell * pitch + start, cell * pitch + start + ROWS)
            from_edge_ref[rows, :] = short_one_hot(across(block, 2 * count), edge_row)
            from_own_ref[rows, :] = short_one_hot(across(block, owned), own_row)

    wide_ref[...] = jnp.zeros_like(wide_ref)
    copy.wait()
    for cell in range(cells):
        wide_ref[cell % 2, :nodes, :nodes] = matrix_ref[cell].astype(f32)
        padded_ref[cell] = wide_ref[cell % 2].astype(bf16)


def store(ref, rows, columns, values):
    ref[rows, columns] = values


def cell_block(values, matrix_ref, cell):
    pitch = matrix_ref.shape[1]
    return dot(values[:, cell * pitch : (cell + 1) * pitch], matrix_ref[cell])


def put_parts(parts_ref, cell, pitch, block):
    parts_ref[:, cell * pitch : (cell + 1) * pitch] = halves(block)


def chosen(flags_ref, first, second):
    even = flags_ref[2] > 0
    return jnp.where(even, second, first), jnp.where(even, first, second)


def cell_values(edge, inner_values_ref, edge_lane, edge_block, cell, pitch):
    tiles = []
    for start in range(cell * pitch, (cell + 1) * pitch, LANES):
        columns = slice(start, start + LANES)
        lane, block = edge_lane[:, columns], edge_block[:, columns]
        tiles.append(
            jnp.concatenate(
                [
                    gathered(
                        edge[row : row + ROWS], lane, block, inner_values_ref[row : row + ROWS, columns]
                    )
                    for row in range(0, edge.shape[0], ROWS)
                ],
                axis=0,
            )
        )
    return jnp.concatenate(tiles, axis=1)


def send_sums(
    flags_ref, edge, inner_values_ref, edge_lane, edge_block, matrix_ref, from_edge_ref,
    parts_ref, first_ref, second_ref,
):
    cells, pitch, _ = matrix_ref.shape
    for cell in range(cells):
        values = cell_values(edge, inner_values_ref, edge_lane, edge_block, cell, pitch)
        parts_ref[:, cell * pitch : (cell + 1) * pitch] = halves(dot(values, matrix_ref[cell]))
    sums = joined(dot(parts_ref[...], from_edge_ref[...]))
    count = first_ref.shape[1]
    first_ref[...], second_ref[...] = chosen(flags_ref, sums[:, :count], sums[:, count:])


def first_kernel(
    flags_ref, inner_values_ref, got_first, got_second, edge_lane, edge_block, matrix_ref, from_edge_ref,
    parts_ref, first_ref, second_ref, state_ref,
):
    got, _ = chosen(flags_ref, got_first[...].astype(f32), got_second[...].astype(f32))
    got = jnp.where(flags_ref[0] > 0, got, jnp.zeros_like(got))
    state_ref[...] = got
    send_sums(
        flags_ref, got.astype(bf16), inner_values_ref, edge_lane, edge_block, matrix_ref, from_edge_ref,
        parts_ref, first_ref, second_ref,
    )


def advance(scale, applied, state, before):
    new = (applied - spectrum_center * state) * scale
    return new if before is None else new - before


def edge_step(scale, flags_ref, got_first, got_second, sum_first, sum_second, ghost, face, before):
    keep_ghost, keep_face = flags_ref[0] > 0, flags_ref[1] > 0
    got_ghost, got_face = chosen(flags_ref, got_first[...], got_second[...])
    sum_ghost, sum_face = chosen(flags_ref, sum_first[...], sum_second[...])
    applied_face = sum_face + jnp.where(keep_face, got_face, jnp.zeros_like(got_face))
    new_face = advance(scale, applied_face, face[...], before and before[1][...])
    new_ghost = advance(scale, sum_ghost + got_ghost, ghost[...], before and before[0][...])
    new_ghost = jnp.where(keep_ghost, new_ghost, jnp.zeros_like(new_ghost))
    return new_ghost, new_face


def edge_values(new_ghost, new_face):
    return jnp.concatenate([new_ghost.astype(bf16), new_face.astype(bf16)], axis=1)


def edge_kernel(scale, with_before, flags_ref, got_first, got_second, sum_first, sum_second, ghost, face, *rest):
    before, rest = (rest[:2], rest[2:]) if with_before else (None, rest)
    inner_values_ref, edge_lane, edge_block, matrix_ref, from_edge_ref, *outs = rest
    parts_ref, out_first, out_second, new_ghost, new_face = outs
    ghost_value, face_value = edge_step(
        scale, flags_ref, got_first, got_second, sum_first, sum_second, ghost, face, before
    )
    new_ghost[...] = ghost_value
    new_face[...] = face_value
    send_sums(
        flags_ref, edge_values(ghost_value, face_value), inner_values_ref, edge_lane, edge_block,
        matrix_ref, from_edge_ref, parts_ref, out_first, out_second,
    )


def inner_kernel(scale, with_before, parts_ref, state_ref, *rest):
    before = rest[0][...] if with_before else None
    own_lane, own_block, from_own_ref, inner_ref, new_ref, values_ref = (
        rest[1:] if with_before else rest
    )
    applied = joined(dot(parts_ref[...], from_own_ref[...]))
    new = advance(scale, applied, state_ref[...], before) * inner_ref[:1]
    new_ref[...] = new
    gather_columns(
        new.astype(bf16), own_lane, own_block, None, functools.partial(store, values_ref)
    )


def density_kernel(
    flags_ref, got_first, got_second, sum_first, sum_second, ghost, face, before_ghost, before_face,
    inner_values_ref, edge_lane, edge_block, basis_ref, occupancy_ref,
    new_face, final_ref, at_ref, band_ref, *, scale, cells,
):
    ghost_value, face_value = edge_step(
        scale, flags_ref, got_first, got_second, sum_first, sum_second, ghost, face,
        (before_ghost, before_face),
    )
    new_face[...] = face_value
    edge = edge_values(ghost_value, face_value)
    nodes = basis_ref.shape[0]
    waves, slots = final_ref.shape
    pitch = slots // cells
    stacked = []
    for cell in range(cells):
        values = cell_values(edge, inner_values_ref, edge_lane, edge_block, cell, pitch)
        final_ref[:, cell * pitch : (cell + 1) * pitch] = values
        stacked.append(values)
    at = dot(jnp.concatenate(stacked, axis=0)[:, :nodes], basis_ref[...])
    at_ref[...] = at
    weights = column(occupancy_ref[...])
    for cell in range(cells):
        block = at[cell * waves : (cell + 1) * waves]
        band_ref[cell : cell + 1, :] = jnp.sum(weights * (block * block), axis=0, keepdims=True)


def products_kernel(
    values_ref, matrix_ref, basis_ref, product_ref, wide_basis_ref, wide_ref
):
    cells, pitch, _ = matrix_ref.shape
    values = values_ref[...]
    for cell in range(cells):
        product_ref[:, cell * pitch : (cell + 1) * pitch] = cell_block(values, matrix_ref, cell)
    nodes = basis_ref.shape[0]
    wide_ref[...] = jnp.zeros_like(wide_ref)
    wide_ref[:nodes, :] = basis_ref[...].astype(f32)
    wide_basis_ref[...] = wide_ref[...].astype(bf16)


def cube_root(x):
    return jnp.exp(jnp.log(x) * (1.0 / 3.0))


def exchange_correlation(density):
    radius = cube_root(0.75 / math.pi / density)
    exchange_part = -cube_root(3.0 / math.pi * density)
    shifted_radius = radius + 7.8
    correlation_part = -0.44 / shifted_radius - 0.44 * radius / (
        3.0 * shifted_radius * shifted_radius
    )
    return exchange_part + correlation_part


def potential_kernel(total_ref, *rest, factor):
    more, (core_ref, quad_ref, at_ref, basis_ref, product_ref, from_edge_ref,
           potential_ref, parts_ref, ghost_ref, twin_ref) = rest[:-10], rest[-10:]
    total = total_ref[...]
    if more:
        total = (total + more[0][...]) + (more[1][...] + more[2][...])
    potential = exchange_correlation(core_ref[...] + factor * total)
    potential_ref[...] = potential
    scaled = quad_ref[...] * potential
    cells = scaled.shape[0]
    waves, slots = product_ref.shape
    pitch = slots // cells
    weighted = jnp.concatenate(
        [
            (at_ref[cell * waves : (cell + 1) * waves, :] * scaled[cell : cell + 1]).astype(bf16)
            for cell in range(cells)
        ],
        axis=0,
    )
    projected = dot_rows(weighted, basis_ref[...])
    for cell in range(cells):
        block = product_ref[:, cell * pitch : (cell + 1) * pitch]
        put_parts(parts_ref, cell, pitch, block + projected[cell * waves : (cell + 1) * waves])
    count = ghost_ref.shape[1]
    sums = joined(dot(parts_ref[...], from_edge_ref[:, :count]))
    ghost_ref[...] = sums
    twin_ref[...] = sums


def residual_kernel(
    parts_ref, state_ref, face_ref, ritz_ref, from_own_ref, potential_ref,
    out_ref, shift_ref, potential_out, sem,
):
    copy = pltpu.make_async_copy(potential_ref, potential_out, sem)
    copy.start()
    ritz = column(ritz_ref[...])
    shift_ref[...] = ritz * face_ref[...]
    out_ref[...] = joined(dot(parts_ref[...], from_own_ref[...])) - ritz * state_ref[...]
    copy.wait()


def finish_kernel(
    flags_ref, got_first, got_second, partial_ref, shift_ref, node_lane, node_block,
    out_ref, hold_ref, sem,
):
    _, got = chosen(flags_ref, got_first[...], got_second[...])
    got = jnp.where(flags_ref[1] > 0, got, jnp.zeros_like(got)) - shift_ref[...]

    def add(rows, columns, values):
        hold_ref[rows, columns] = partial_ref[rows, columns] + values

    gather_columns(got, node_lane, node_block, None, add)
    copy = pltpu.make_async_copy(hold_ref, out_ref, sem)
    copy.start()
    copy.wait()


def paired(x, parity):
    domains, bands = lax.axis_size("space"), lax.axis_size("band")
    route = []
    for domain in range(domains):
        other = domain + 1 if domain % 2 == parity else domain - 1
        for band in range(bands):
            target = (other, band) if 0 <= other < domains else (domain, band ^ 1 if bands % 2 == 0 else band)
            route.append((domain * bands + band, target[0] * bands + target[1]))
    return lax.ppermute(x, ("space", "band"), route)


def exchanged(first, second):
    return paired(first, 0), paired(second, 1)


def swapped(x, axis, mask):
    return lax.ppermute(x, axis, [(i, i ^ mask) for i in range(lax.axis_size(axis))])


def band_parts(x, axis):
    count = lax.axis_size(axis)
    if count & (count - 1):
        return [lax.psum(x, axis)]
    bit = 1
    if count > 1:
        x = x + swapped(x, axis, bit)
        bit = 2
    parts = [x]
    while bit < count:
        x = parts[0] if len(parts) == 1 else (parts[0] + parts[1]) + (parts[2] + parts[3])
        if 2 * bit < count:
            parts = [x] + [swapped(x, axis, mask ^ 1) for mask in (bit, 2 * bit, 3 * bit)]
            bit *= 4
        else:
            parts = [x + swapped(x, axis, bit ^ 1)]
            bit *= 2
    return parts


def shards(
    wavefunctions,
    cell_hamiltonian,
    connectivity,
    face_nodes,
    basis_values,
    quad_weights,
    core_density,
    occupancy,
    ritz_values,
):
    waves, owned = wavefunctions.shape
    count = face_nodes.shape[0]
    cells, nodes = connectivity.shape
    points = basis_values.shape[1]
    pitch = -(-nodes // 128) * 128
    slots = cells * pitch
    band_total = waves * lax.axis_size("band")
    domain = lax.axis_index("space")
    flags = jnp.stack(
        [domain > 0, domain < lax.axis_size("space") - 1, domain % 2 == 0]
    ).astype(jnp.int32)
    edge_out = [((waves, count), f32)] * 2
    parts_out = ((2 * waves, slots), bf16)
    values_out = ((waves, slots), bf16)
    state_out = ((waves, owned), f32)

    index_out = ((ROWS, slots), jnp.int16)
    w, faces, links, start_face, start_twin = call(
        pick_kernel,
        [
            (wavefunctions.shape, bf16),
            ((1, count), jnp.int32),
            (connectivity.shape, jnp.int32),
            ((waves, count), bf16),
            ((waves, count), bf16),
        ],
        wavefunctions, face_nodes.reshape(1, count), connectivity,
        held=3, scratch=[pltpu.SemaphoreType.DMA((3,))], room=56,
    )
    start_pair = exchanged(start_twin, start_face)
    (
        from_own, from_edge, padded, own_lane, own_block, edge_lane, edge_block,
        node_lane, node_block, inner, values, state,
    ) = call(
        tables_kernel,
        [
            ((slots, owned), bf16),
            ((slots, 2 * count), bf16),
            ((cells, pitch, pitch), bf16),
            *[index_out] * 4,
            ((ROWS // 2, owned), jnp.int32),
            ((ROWS // 2, owned), jnp.int32),
            ((ROWS // 2, owned), f32),
            values_out,
            state_out,
        ],
        cell_hamiltonian, w, faces, links,
        held=1,
        scratch=[
            pltpu.VMEM((ROWS // 2, slots), jnp.int32),
            pltpu.VMEM((-(-cells // LANES) * LANES, pitch), f32),
            pltpu.VMEM((2, pitch, pitch), f32),
            pltpu.VMEM((owned, count), bf16),
            pltpu.VMEM(cell_hamiltonian.shape, bf16),
            pltpu.SemaphoreType.DMA,
        ],
        room=44,
    )
    parts, *sums, ghost = call(
        first_kernel,
        [parts_out, *edge_out, edge_out[0]],
        flags, values, *start_pair, edge_lane, edge_block, padded, from_edge, smem=1,
    )
    face = start_face.astype(f32)
    before_edge, before_state = (), ()
    scale = 1.0 / spectrum_half
    for step in range(3):
        got = exchanged(*sums)
        new_state, values = call(
            functools.partial(inner_kernel, scale, step > 0),
            [state_out, values_out],
            parts, state, *before_state, own_lane, own_block, from_own, inner,
        )
        received = (flags, *got, *sums, ghost, face, *before_edge)
        if step < 2:
            parts, *sums, new_ghost, new_face = call(
                functools.partial(edge_kernel, scale, step > 0),
                [parts_out, *edge_out, *edge_out],
                *received, values, edge_lane, edge_block, padded, from_edge, smem=1,
            )
            before_edge, ghost, face = (ghost, face), new_ghost, new_face
        else:
            face, final, at, band = call(
                functools.partial(density_kernel, scale=scale, cells=cells),
                [edge_out[0], values_out, ((cells * waves, points), f32), ((cells, points), f32)],
                *received, values, edge_lane, edge_block, basis_values, occupancy.reshape(1, waves), smem=1,
            )
        before_state, state = (state,), new_state
        scale = 2.0 / spectrum_half
    products, wide_basis = call(
        products_kernel,
        [((waves, slots), f32), ((pitch, points), bf16)],
        final, padded, basis_values, scratch=[pltpu.VMEM((pitch, points), f32)],
    )
    totals = band_parts(band, "band")
    potential, parts, *sums = call(
        functools.partial(potential_kernel, factor=2.0 / band_total),
        [((cells, points), f32), parts_out, *edge_out],
        *totals, core_density, quad_weights, at, wide_basis, products, from_edge,
    )
    returned = exchanged(*sums)
    partial, shift, potential = call(
        residual_kernel,
        [state_out, edge_out[0], ((cells, points), f32)],
        parts, state, face, ritz_values.reshape(1, waves), from_own, potential,
        sent=1, scratch=[pltpu.SemaphoreType.DMA],
    )
    (residual,) = call(
        finish_kernel, [state_out], flags, *returned, partial, shift, node_lane, node_block,
        smem=1, sent=1, scratch=[pltpu.VMEM(*state_out), pltpu.SemaphoreType.DMA],
    )
    return (residual, potential)


def solution(mesh):
    in_specs = (
        P("band", "space"),
        P("space", None, None),
        P("space", None),
        P("space"),
        P(),
        P("space", None),
        P("space", None),
        P("band"),
        P("band"),
    )
    out_specs = (P("band", "space"), P("space", None))
    return jax.shard_map(shards, mesh=mesh, in_specs=in_specs, out_specs=out_specs, check_vma=False)
```

```python
import functools
import math

import jax
import jax.numpy as jnp
from jax import lax
from jax.experimental import pallas as pl
from jax.experimental.pallas import tpu as pltpu
from jax.sharding import PartitionSpec as P

spectrum_center = 5.0
spectrum_half = 5.5

VMEM = pl.BlockSpec(memory_space=pltpu.VMEM)
SMEM = pl.BlockSpec(memory_space=pltpu.SMEM)
OUTSIDE = pl.BlockSpec(memory_space=pltpu.HBM)
bf16 = jnp.bfloat16
f32 = jnp.float32


def dot(left, right):
    return jnp.dot(left, right, preferred_element_type=f32)


def dot_rows(left, right):
    return lax.dot_general(left, right, (((1,), (1,)), ((), ())), preferred_element_type=f32)


def halves(x):
    high = x.astype(bf16)
    low = (x - high.astype(f32)).astype(bf16)
    return jnp.concatenate([high, low], axis=0)


def joined(x):
    rows = x.shape[0] // 2
    return x[:rows] + x[rows:]


def column(row):
    n = row.shape[1]
    eye = lax.broadcasted_iota(jnp.int32, (n, n), 0) == lax.broadcasted_iota(jnp.int32, (n, n), 1)
    return jnp.sum(jnp.where(eye, row, jnp.zeros_like(row)), axis=1, keepdims=True)


def one_hot(hit):
    return jnp.where(hit, 1.0, 0.0).astype(bf16)


def call(kernel, outs, *args, flops=1 << 28, smem=0, held=0, sent=0, scratch=(), room=20):
    count = len(args) - smem - held
    kept = len(outs) - sent
    return pl.pallas_call(
        kernel,
        out_shape=[pltpu.VMEM(*out) for out in outs[:kept]]
        + [jax.ShapeDtypeStruct(*out) for out in outs[kept:]],
        in_specs=[SMEM] * smem + [OUTSIDE] * held + [VMEM] * count,
        out_specs=[VMEM] * kept + [OUTSIDE] * sent,
        scratch_shapes=list(scratch),
        compiler_params=pltpu.CompilerParams(vmem_limit_bytes=room << 20),
        cost_estimate=pl.CostEstimate(flops=flops, bytes_accessed=1 << 20, transcendentals=0),
    )(*args)


LANES = 128
ROWS = 16
ALONG = lax.GatherDimensionNumbers(
    offset_dims=(),
    collapsed_slice_dims=(1,),
    start_index_map=(1,),
    operand_batching_dims=(0,),
    start_indices_batching_dims=(0,),
)


def along(block, lane):
    return lax.gather(
        block, lane[..., None], ALONG, slice_sizes=(1, 1),
        mode=lax.GatherScatterMode.PROMISE_IN_BOUNDS,
    )


def gathered(source, lane, block, start=None, before=0):
    out = jnp.zeros(lane.shape, source.dtype) if start is None else start
    for number in range(source.shape[1] // LANES):
        part = along(source[:, number * LANES : (number + 1) * LANES], lane)
        out = jnp.where(block == number - before, part, out)
    return out


def gather_columns(source, lane_ref, block_ref, start, put):
    rows = lane_ref.shape[0]
    for column_start in range(0, lane_ref.shape[1], LANES):
        columns = slice(column_start, column_start + LANES)
        lane, block = lane_ref[:, columns], block_ref[:, columns]
        for row in range(0, source.shape[0], rows):
            begin = None if start is None else start[row : row + rows, columns]
            put(slice(row, row + rows), columns, gathered(source[row : row + rows], lane, block, begin))


def split_index(index, dtype):
    return (index & (LANES - 1)).astype(dtype), (index >> 7).astype(dtype)


def pick_kernel(w_in, face_in, links_in, w_ref, face_ref, links_ref, out_ref, twin_ref, sems):
    pairs = ((w_in, w_ref), (face_in, face_ref), (links_in, links_ref))
    copies = [
        pltpu.make_async_copy(source, target, sems.at[i]) for i, (source, target) in enumerate(pairs)
    ]
    for copy in copies:
        copy.start()
    for copy in copies:
        copy.wait()
    count = face_ref.shape[1]
    w = w_ref[...]
    for start in range(0, count, LANES):
        index = jnp.broadcast_to(face_ref[:, start : start + LANES], (ROWS, LANES))
        lane, block = split_index(index, jnp.int16)
        for row in range(0, w.shape[0], ROWS):
            picked = gathered(w[row : row + ROWS], lane, block)
            out_ref[row : row + ROWS, start : start + LANES] = picked
            twin_ref[row : row + ROWS, start : start + LANES] = picked


def short_one_hot(left, right):
    return jnp.where(left == right, jnp.ones(left.shape, bf16), jnp.zeros(left.shape, bf16))


def across(block, width):
    return jnp.concatenate([block] * (width // block.shape[1]), axis=1)


def tables_kernel(
    matrix_in, w_ref, face_ref, links_ref,
    from_own_ref, from_edge_ref, padded_ref, own_lane, own_block, values_ref,
    row_ref, turn_ref, wide_ref, matrix_ref, sem,
):
    copy = pltpu.make_async_copy(matrix_in, matrix_ref, sem)
    copy.start()
    slots, owned = from_own_ref.shape
    count = face_ref.shape[1]
    cells, nodes = links_ref.shape
    pitch = slots // cells
    short = jnp.int16

    row_ref[...] = jnp.full(row_ref.shape, -1, jnp.int32)
    turn_ref[...] = jnp.full(turn_ref.shape, -1.0, f32)
    for cell in range(cells):
        line = links_ref[cell : cell + 1, :]
        row_ref[:, cell * pitch : cell * pitch + nodes] = jnp.broadcast_to(line, (ROWS, nodes))
        turn_ref[cell : cell + 1, :nodes] = line.astype(f32)

    for start in range(0, slots, LANES):
        columns = slice(start, start + LANES)
        own_lane[:, columns], own_block[:, columns] = split_index(row_ref[:, columns] - count, short)
    w = w_ref[...]
    gather_columns(w, own_lane, own_block, None, functools.partial(store, values_ref))

    edge_row = jnp.concatenate(
        [
            lax.broadcasted_iota(jnp.int32, (ROWS, count), 1),
            jnp.broadcast_to(face_ref[...], (ROWS, count)) + count,
        ],
        axis=1,
    ).astype(short)
    own_row = (lax.broadcasted_iota(jnp.int32, (ROWS, owned), 1) + count).astype(short)
    turned = jnp.transpose(turn_ref[...])
    for cell in range(cells):
        for start in range(0, pitch, ROWS):
            block = jnp.broadcast_to(turned[start : start + ROWS, cell : cell + 1], (ROWS, LANES))
            block = block.astype(jnp.int32).astype(short)
            rows = slice(cell * pitch + start, cell * pitch + start + ROWS)
            from_edge_ref[rows, :] = short_one_hot(across(block, 2 * count), edge_row)
            from_own_ref[rows, :] = short_one_hot(across(block, owned), own_row)

    wide_ref[...] = jnp.zeros_like(wide_ref)
    copy.wait()
    for cell in range(cells):
        wide_ref[cell % 2, :nodes, :nodes] = matrix_ref[cell].astype(f32)
        padded_ref[cell] = wide_ref[cell % 2].astype(bf16)


def store(ref, rows, columns, values):
    ref[rows, columns] = values


def cell_block(values, matrix_ref, cell):
    pitch = matrix_ref.shape[1]
    return dot(values[:, cell * pitch : (cell + 1) * pitch], matrix_ref[cell])


def put_parts(parts_ref, cell, pitch, block):
    parts_ref[:, cell * pitch : (cell + 1) * pitch] = halves(block)


def chosen(flags_ref, first, second):
    even = flags_ref[2] > 0
    return jnp.where(even, second, first), jnp.where(even, first, second)


def cell_values(edge, inner_values_ref, edge_lane, edge_block, cell, pitch, before=0):
    tiles = []
    for start in range(cell * pitch, (cell + 1) * pitch, LANES):
        columns = slice(start, start + LANES)
        lane, block = edge_lane[:, columns], edge_block[:, columns]
        tiles.append(
            jnp.concatenate(
                [
                    gathered(
                        edge[row : row + ROWS], lane, block,
                        inner_values_ref[row : row + ROWS, columns], before,
                    )
                    for row in range(0, edge.shape[0], ROWS)
                ],
                axis=0,
            )
        )
    return jnp.concatenate(tiles, axis=1)


def send_sums(
    flags_ref, edge, inner_values_ref, edge_lane, edge_block, matrix_ref, from_edge_ref,
    parts_ref, first_ref, second_ref, before=0,
):
    cells, pitch, _ = matrix_ref.shape
    for cell in range(cells):
        values = cell_values(edge, inner_values_ref, edge_lane, edge_block, cell, pitch, before)
        parts_ref[:, cell * pitch : (cell + 1) * pitch] = halves(dot(values, matrix_ref[cell]))
    sums = joined(dot(parts_ref[...], from_edge_ref[...]))
    count = first_ref.shape[1]
    first_ref[...], second_ref[...] = chosen(flags_ref, sums[:, :count], sums[:, count:])


def first_kernel(
    flags_ref, inner_values_ref, got_first, got_second, own_lane, own_block, matrix_ref, from_edge_ref,
    parts_ref, first_ref, second_ref, state_ref,
):
    got, _ = chosen(flags_ref, got_first[...].astype(f32), got_second[...].astype(f32))
    got = jnp.where(flags_ref[0] > 0, got, jnp.zeros_like(got))
    state_ref[...] = got
    send_sums(
        flags_ref, got.astype(bf16), inner_values_ref, own_lane, own_block, matrix_ref, from_edge_ref,
        parts_ref, first_ref, second_ref, before=got.shape[1] // LANES,
    )


def advance(scale, applied, state, before):
    new = (applied - spectrum_center * state) * scale
    return new if before is None else new - before


def edge_step(scale, flags_ref, got_first, got_second, sum_first, sum_second, ghost, face, before):
    keep_ghost, keep_face = flags_ref[0] > 0, flags_ref[1] > 0
    got_ghost, got_face = chosen(flags_ref, got_first[...], got_second[...])
    sum_ghost, sum_face = chosen(flags_ref, sum_first[...], sum_second[...])
    applied_face = sum_face + jnp.where(keep_face, got_face, jnp.zeros_like(got_face))
    new_face = advance(scale, applied_face, face[...], before and before[1][...])
    new_ghost = advance(scale, sum_ghost + got_ghost, ghost[...], before and before[0][...])
    new_ghost = jnp.where(keep_ghost, new_ghost, jnp.zeros_like(new_ghost))
    return new_ghost, new_face


def edge_values(new_ghost, new_face):
    return jnp.concatenate([new_ghost.astype(bf16), new_face.astype(bf16)], axis=1)


def edge_kernel(scale, with_before, flags_ref, got_first, got_second, sum_first, sum_second, ghost, face, *rest):
    before, rest = (rest[:2], rest[2:]) if with_before else (None, rest)
    inner_values_ref, edge_lane, edge_block, matrix_ref, from_edge_ref, *outs = rest
    parts_ref, out_first, out_second, new_ghost, new_face = outs
    ghost_value, face_value = edge_step(
        scale, flags_ref, got_first, got_second, sum_first, sum_second, ghost, face, before
    )
    new_ghost[...] = ghost_value
    new_face[...] = face_value
    send_sums(
        flags_ref, edge_values(ghost_value, face_value), inner_values_ref, edge_lane, edge_block,
        matrix_ref, from_edge_ref, parts_ref, out_first, out_second,
    )


def start_kernel(
    scale, parts_ref, w_ref, face_ref, own_lane, own_block, from_own_ref,
    new_ref, values_ref, state_ref, inner_ref, node_lane, node_block, edge_lane, edge_block, table_ref,
):
    slots, owned = from_own_ref.shape
    count = face_ref.shape[1]
    half = ROWS // 2
    table_ref[...] = one_hot(lax.broadcasted_iota(jnp.int32, (owned, count), 0) == face_ref[...])
    order = lax.broadcasted_iota(jnp.int32, (half, count), 1)
    digits = jnp.concatenate([order >> 7, (order & (LANES - 1)) + 1], axis=0)
    sums = dot_rows(digits.astype(f32).astype(bf16), table_ref[...])

    applied = joined(dot(parts_ref[...], from_own_ref[...]))
    place = sums[:half] * float(LANES) + sums[half:]
    node_lane[...], node_block[...] = split_index(place.astype(jnp.int32) - 1, jnp.int32)
    inner = jnp.where(place > 0.5, 0.0, 1.0)
    inner_ref[...] = inner
    state = w_ref[...].astype(f32) * inner[:1]
    state_ref[...] = state
    new = advance(scale, applied, state, None) * inner[:1]
    new_ref[...] = new
    gather_columns(
        new.astype(bf16), own_lane, own_block, None, functools.partial(store, values_ref)
    )

    short_sums = sums.astype(bf16)
    for start in range(0, slots, LANES):
        columns = slice(start, start + LANES)
        at_face = gathered(short_sums, own_lane[:, columns], own_block[:, columns]).astype(f32)
        at_face = (at_face[:half] * float(LANES) + at_face[half:]).astype(jnp.int32)
        index = own_block[:half, columns].astype(jnp.int32) * LANES + own_lane[:half, columns].astype(jnp.int32)
        index = index + count
        index = jnp.where(index < count, index, jnp.where(at_face > 0, at_face + (count - 1), -1))
        lane, block = split_index(jnp.concatenate([index, index], axis=0), jnp.int16)
        edge_lane[:, columns] = lane
        edge_block[:, columns] = block


def inner_kernel(
    scale, parts_ref, state_ref, before_ref, own_lane, own_block, from_own_ref, inner_ref,
    new_ref, values_ref,
):
    applied = joined(dot(parts_ref[...], from_own_ref[...]))
    new = advance(scale, applied, state_ref[...], before_ref[...]) * inner_ref[:1]
    new_ref[...] = new
    gather_columns(
        new.astype(bf16), own_lane, own_block, None, functools.partial(store, values_ref)
    )


def density_kernel(
    flags_ref, got_first, got_second, sum_first, sum_second, ghost, face, before_ghost, before_face,
    inner_values_ref, edge_lane, edge_block, basis_ref, occupancy_ref,
    new_face, final_ref, at_ref, band_ref, *, scale, cells,
):
    ghost_value, face_value = edge_step(
        scale, flags_ref, got_first, got_second, sum_first, sum_second, ghost, face,
        (before_ghost, before_face),
    )
    new_face[...] = face_value
    edge = edge_values(ghost_value, face_value)
    nodes = basis_ref.shape[0]
    waves, slots = final_ref.shape
    pitch = slots // cells
    stacked = []
    for cell in range(cells):
        values = cell_values(edge, inner_values_ref, edge_lane, edge_block, cell, pitch)
        final_ref[:, cell * pitch : (cell + 1) * pitch] = values
        stacked.append(values)
    at = dot(jnp.concatenate(stacked, axis=0)[:, :nodes], basis_ref[...])
    at_ref[...] = at
    weights = column(occupancy_ref[...])
    for cell in range(cells):
        block = at[cell * waves : (cell + 1) * waves]
        band_ref[cell : cell + 1, :] = jnp.sum(weights * (block * block), axis=0, keepdims=True)


def products_kernel(
    values_ref, matrix_ref, basis_ref, product_ref, wide_basis_ref, wide_ref
):
    cells, pitch, _ = matrix_ref.shape
    values = values_ref[...]
    for cell in range(cells):
        product_ref[:, cell * pitch : (cell + 1) * pitch] = cell_block(values, matrix_ref, cell)
    nodes = basis_ref.shape[0]
    wide_ref[...] = jnp.zeros_like(wide_ref)
    wide_ref[:nodes, :] = basis_ref[...].astype(f32)
    wide_basis_ref[...] = wide_ref[...].astype(bf16)


def cube_root(x):
    return jnp.exp(jnp.log(x) * (1.0 / 3.0))


def exchange_correlation(density):
    radius = cube_root(0.75 / math.pi / density)
    exchange_part = -cube_root(3.0 / math.pi * density)
    shifted_radius = radius + 7.8
    correlation_part = -0.44 / shifted_radius - 0.44 * radius / (
        3.0 * shifted_radius * shifted_radius
    )
    return exchange_part + correlation_part


def potential_kernel(total_ref, *rest, factor):
    more, (core_ref, quad_ref, at_ref, basis_ref, product_ref, from_edge_ref,
           potential_ref, parts_ref, ghost_ref, twin_ref) = rest[:-10], rest[-10:]
    total = total_ref[...]
    if more:
        total = (total + more[0][...]) + (more[1][...] + more[2][...])
    potential = exchange_correlation(core_ref[...] + factor * total)
    potential_ref[...] = potential
    scaled = quad_ref[...] * potential
    cells = scaled.shape[0]
    waves, slots = product_ref.shape
    pitch = slots // cells
    weighted = jnp.concatenate(
        [
            (at_ref[cell * waves : (cell + 1) * waves, :] * scaled[cell : cell + 1]).astype(bf16)
            for cell in range(cells)
        ],
        axis=0,
    )
    projected = dot_rows(weighted, basis_ref[...])
    for cell in range(cells):
        block = product_ref[:, cell * pitch : (cell + 1) * pitch]
        put_parts(parts_ref, cell, pitch, block + projected[cell * waves : (cell + 1) * waves])
    count = ghost_ref.shape[1]
    sums = joined(dot(parts_ref[...], from_edge_ref[:, :count]))
    ghost_ref[...] = sums
    twin_ref[...] = sums


def residual_kernel(
    parts_ref, state_ref, face_ref, ritz_ref, from_own_ref, potential_ref,
    out_ref, shift_ref, potential_out, sem,
):
    copy = pltpu.make_async_copy(potential_ref, potential_out, sem)
    copy.start()
    ritz = column(ritz_ref[...])
    shift_ref[...] = ritz * face_ref[...]
    out_ref[...] = joined(dot(parts_ref[...], from_own_ref[...])) - ritz * state_ref[...]
    copy.wait()


def finish_kernel(
    flags_ref, got_first, got_second, partial_ref, shift_ref, node_lane, node_block,
    out_ref, hold_ref, sem,
):
    _, got = chosen(flags_ref, got_first[...], got_second[...])
    got = jnp.where(flags_ref[1] > 0, got, jnp.zeros_like(got)) - shift_ref[...]

    def add(rows, columns, values):
        hold_ref[rows, columns] = partial_ref[rows, columns] + values

    gather_columns(got, node_lane, node_block, None, add)
    copy = pltpu.make_async_copy(hold_ref, out_ref, sem)
    copy.start()
    copy.wait()


def paired(x, parity):
    domains, bands = lax.axis_size("space"), lax.axis_size("band")
    route = []
    for domain in range(domains):
        other = domain + 1 if domain % 2 == parity else domain - 1
        for band in range(bands):
            target = (other, band) if 0 <= other < domains else (domain, band ^ 1 if bands % 2 == 0 else band)
            route.append((domain * bands + band, target[0] * bands + target[1]))
    return lax.ppermute(x, ("space", "band"), route)


def exchanged(first, second):
    return paired(first, 0), paired(second, 1)


def swapped(x, axis, mask):
    return lax.ppermute(x, axis, [(i, i ^ mask) for i in range(lax.axis_size(axis))])


def band_parts(x, axis):
    count = lax.axis_size(axis)
    if count & (count - 1):
        return [lax.psum(x, axis)]
    bit = 1
    if count > 1:
        x = x + swapped(x, axis, bit)
        bit = 2
    parts = [x]
    while bit < count:
        x = parts[0] if len(parts) == 1 else (parts[0] + parts[1]) + (parts[2] + parts[3])
        if 2 * bit < count:
            parts = [x] + [swapped(x, axis, mask ^ 1) for mask in (bit, 2 * bit, 3 * bit)]
            bit *= 4
        else:
            parts = [x + swapped(x, axis, bit ^ 1)]
            bit *= 2
    return parts


def shards(
    wavefunctions,
    cell_hamiltonian,
    connectivity,
    face_nodes,
    basis_values,
    quad_weights,
    core_density,
    occupancy,
    ritz_values,
):
    waves, owned = wavefunctions.shape
    count = face_nodes.shape[0]
    cells, nodes = connectivity.shape
    points = basis_values.shape[1]
    pitch = -(-nodes // 128) * 128
    slots = cells * pitch
    band_total = waves * lax.axis_size("band")
    domain = lax.axis_index("space")
    flags = jnp.stack(
        [domain > 0, domain < lax.axis_size("space") - 1, domain % 2 == 0]
    ).astype(jnp.int32)
    edge_out = [((waves, count), f32)] * 2
    parts_out = ((2 * waves, slots), bf16)
    values_out = ((waves, slots), bf16)
    state_out = ((waves, owned), f32)

    index_out = ((ROWS, slots), jnp.int16)
    w, faces, links, start_face, start_twin = call(
        pick_kernel,
        [
            (wavefunctions.shape, bf16),
            ((1, count), jnp.int32),
            (connectivity.shape, jnp.int32),
            ((waves, count), bf16),
            ((waves, count), bf16),
        ],
        wavefunctions, face_nodes.reshape(1, count), connectivity,
        held=3, scratch=[pltpu.SemaphoreType.DMA((3,))], room=56,
    )
    start_pair = exchanged(start_twin, start_face)
    (
        from_own, from_edge, padded, own_lane, own_block, values
    ) = call(
        tables_kernel,
        [
            ((slots, owned), bf16),
            ((slots, 2 * count), bf16),
            ((cells, pitch, pitch), bf16),
            *[index_out] * 2,
            values_out,
        ],
        cell_hamiltonian, w, faces, links,
        held=1,
        scratch=[
            pltpu.VMEM((ROWS, slots), jnp.int32),
            pltpu.VMEM((-(-cells // LANES) * LANES, pitch), f32),
            pltpu.VMEM((2, pitch, pitch), f32),
            pltpu.VMEM(cell_hamiltonian.shape, bf16),
            pltpu.SemaphoreType.DMA,
        ],
        room=44,
    )
    parts, *sums, ghost = call(
        first_kernel,
        [parts_out, *edge_out, edge_out[0]],
        flags, values, *start_pair, own_lane, own_block, padded, from_edge, smem=1,
    )
    face = start_face.astype(f32)
    before_edge = ()
    scale = 1.0 / spectrum_half
    for step in range(3):
        got = exchanged(*sums)
        if step == 0:
            (
                new_state, values, state, inner, node_lane, node_block, edge_lane, edge_block
            ) = call(
                functools.partial(start_kernel, scale),
                [
                    state_out,
                    values_out,
                    state_out,
                    ((ROWS // 2, owned), f32),
                    ((ROWS // 2, owned), jnp.int32),
                    ((ROWS // 2, owned), jnp.int32),
                    *[index_out] * 2,
                ],
                parts, w, faces, own_lane, own_block, from_own,
                scratch=[pltpu.VMEM((owned, count), bf16)],
            )
        else:
            new_state, values = call(
                functools.partial(inner_kernel, scale),
                [state_out, values_out],
                parts, state, before_state, own_lane, own_block, from_own, inner,
            )
        received = (flags, *got, *sums, ghost, face, *before_edge)
        if step < 2:
            parts, *sums, new_ghost, new_face = call(
                functools.partial(edge_kernel, scale, step > 0),
                [parts_out, *edge_out, *edge_out],
                *received, values, edge_lane, edge_block, padded, from_edge, smem=1,
            )
            before_edge, ghost, face = (ghost, face), new_ghost, new_face
        else:
            face, final, at, band = call(
                functools.partial(density_kernel, scale=scale, cells=cells),
                [edge_out[0], values_out, ((cells * waves, points), f32), ((cells, points), f32)],
                *received, values, edge_lane, edge_block, basis_values, occupancy.reshape(1, waves), smem=1,
            )
        before_state, state = state, new_state
        scale = 2.0 / spectrum_half
    products, wide_basis = call(
        products_kernel,
        [((waves, slots), f32), ((pitch, points), bf16)],
        final, padded, basis_values, scratch=[pltpu.VMEM((pitch, points), f32)],
    )
    totals = band_parts(band, "band")
    potential, parts, *sums = call(
        functools.partial(potential_kernel, factor=2.0 / band_total),
        [((cells, points), f32), parts_out, *edge_out],
        *totals, core_density, quad_weights, at, wide_basis, products, from_edge,
    )
    returned = exchanged(*sums)
    partial, shift, potential = call(
        residual_kernel,
        [state_out, edge_out[0], ((cells, points), f32)],
        parts, state, face, ritz_values.reshape(1, waves), from_own, potential,
        sent=1, scratch=[pltpu.SemaphoreType.DMA],
    )
    (residual,) = call(
        finish_kernel, [state_out], flags, *returned, partial, shift, node_lane, node_block,
        smem=1, sent=1, scratch=[pltpu.VMEM(*state_out), pltpu.SemaphoreType.DMA],
    )
    return (residual, potential)


def solution(mesh):
    in_specs = (
        P("band", "space"),
        P("space", None, None),
        P("space", None),
        P("space"),
        P(),
        P("space", None),
        P("space", None),
        P("band"),
        P("band"),
    )
    out_specs = (P("band", "space"), P("space", None))
    return jax.shard_map(shards, mesh=mesh, in_specs=in_specs, out_specs=out_specs, check_vma=False)
```

```python
import functools
import math

import jax
import jax.numpy as jnp
from jax import lax
from jax.experimental import pallas as pl
from jax.experimental.pallas import tpu as pltpu
from jax.sharding import PartitionSpec as P

spectrum_center = 5.0
spectrum_half = 5.5

VMEM = pl.BlockSpec(memory_space=pltpu.VMEM)
SMEM = pl.BlockSpec(memory_space=pltpu.SMEM)
OUTSIDE = pl.BlockSpec(memory_space=pltpu.HBM)
bf16 = jnp.bfloat16
f32 = jnp.float32


def dot(left, right):
    return jnp.dot(left, right, preferred_element_type=f32)


def dot_rows(left, right):
    return lax.dot_general(left, right, (((1,), (1,)), ((), ())), preferred_element_type=f32)


def halves(x):
    high = x.astype(bf16)
    low = (x - high.astype(f32)).astype(bf16)
    return jnp.concatenate([high, low], axis=0)


def joined(x):
    rows = x.shape[0] // 2
    return x[:rows] + x[rows:]


def column(row):
    n = row.shape[1]
    eye = lax.broadcasted_iota(jnp.int32, (n, n), 0) == lax.broadcasted_iota(jnp.int32, (n, n), 1)
    return jnp.sum(jnp.where(eye, row, jnp.zeros_like(row)), axis=1, keepdims=True)


def one_hot(hit):
    return jnp.where(hit, 1.0, 0.0).astype(bf16)


def call(kernel, outs, *args, flops=1 << 28, smem=0, held=0, sent=0, scratch=(), room=20):
    count = len(args) - smem - held
    kept = len(outs) - sent
    return pl.pallas_call(
        kernel,
        out_shape=[pltpu.VMEM(*out) for out in outs[:kept]]
        + [jax.ShapeDtypeStruct(*out) for out in outs[kept:]],
        in_specs=[SMEM] * smem + [OUTSIDE] * held + [VMEM] * count,
        out_specs=[VMEM] * kept + [OUTSIDE] * sent,
        scratch_shapes=list(scratch),
        compiler_params=pltpu.CompilerParams(vmem_limit_bytes=room << 20),
        cost_estimate=pl.CostEstimate(flops=flops, bytes_accessed=1 << 20, transcendentals=0),
    )(*args)


LANES = 128
ROWS = 16
ALONG = lax.GatherDimensionNumbers(
    offset_dims=(),
    collapsed_slice_dims=(1,),
    start_index_map=(1,),
    operand_batching_dims=(0,),
    start_indices_batching_dims=(0,),
)


def along(block, lane):
    return lax.gather(
        block, lane[..., None], ALONG, slice_sizes=(1, 1),
        mode=lax.GatherScatterMode.PROMISE_IN_BOUNDS,
    )


def gathered(source, lane, block, start=None, before=0):
    out = jnp.zeros(lane.shape, source.dtype) if start is None else start
    for number in range(source.shape[1] // LANES):
        part = along(source[:, number * LANES : (number + 1) * LANES], lane)
        out = jnp.where(block == number - before, part, out)
    return out


def gather_columns(source, lane_ref, block_ref, start, put):
    rows = lane_ref.shape[0]
    for column_start in range(0, lane_ref.shape[1], LANES):
        columns = slice(column_start, column_start + LANES)
        lane, block = lane_ref[:, columns], block_ref[:, columns]
        for row in range(0, source.shape[0], rows):
            begin = None if start is None else start[row : row + rows, columns]
            put(slice(row, row + rows), columns, gathered(source[row : row + rows], lane, block, begin))


def split_index(index, dtype):
    return (index & (LANES - 1)).astype(dtype), (index >> 7).astype(dtype)


def pick_kernel(w_in, face_in, links_in, w_ref, face_ref, links_ref, out_ref, twin_ref, sems):
    pairs = ((w_in, w_ref), (face_in, face_ref), (links_in, links_ref))
    copies = [
        pltpu.make_async_copy(source, target, sems.at[i]) for i, (source, target) in enumerate(pairs)
    ]
    for copy in copies:
        copy.start()
    for copy in copies:
        copy.wait()
    count = face_ref.shape[1]
    w = w_ref[...]
    for start in range(0, count, LANES):
        index = jnp.broadcast_to(face_ref[:, start : start + LANES], (ROWS, LANES))
        lane, block = split_index(index, jnp.int16)
        for row in range(0, w.shape[0], ROWS):
            picked = gathered(w[row : row + ROWS], lane, block)
            out_ref[row : row + ROWS, start : start + LANES] = picked
            twin_ref[row : row + ROWS, start : start + LANES] = picked


def short_one_hot(left, right):
    return jnp.where(left == right, jnp.ones(left.shape, bf16), jnp.zeros(left.shape, bf16))


def across(block, width):
    return jnp.concatenate([block] * (width // block.shape[1]), axis=1)


def tables_kernel(
    matrix_in, w_ref, face_ref, links_ref,
    from_own_ref, from_edge_ref, padded_ref, own_lane, own_block, values_ref,
    row_ref, turn_ref, wide_ref, matrix_ref, sem,
):
    copy = pltpu.make_async_copy(matrix_in, matrix_ref, sem)
    copy.start()
    slots, owned = from_own_ref.shape
    count = face_ref.shape[1]
    cells, nodes = links_ref.shape
    pitch = slots // cells
    short = jnp.int16

    row_ref[...] = jnp.full(row_ref.shape, -1, jnp.int32)
    turn_ref[...] = jnp.full(turn_ref.shape, -1.0, f32)
    for cell in range(cells):
        line = links_ref[cell : cell + 1, :]
        row_ref[:, cell * pitch : cell * pitch + nodes] = jnp.broadcast_to(line, (ROWS, nodes))
        turn_ref[cell : cell + 1, :nodes] = line.astype(f32)

    edge_row = jnp.concatenate(
        [
            lax.broadcasted_iota(jnp.int32, (ROWS, count), 1),
            jnp.broadcast_to(face_ref[...], (ROWS, count)) + count,
        ],
        axis=1,
    ).astype(short)
    own_row = (lax.broadcasted_iota(jnp.int32, (ROWS, owned), 1) + count).astype(short)
    turned = jnp.transpose(turn_ref[...])
    for cell in range(cells):
        for start in range(0, pitch, ROWS):
            block = jnp.broadcast_to(turned[start : start + ROWS, cell : cell + 1], (ROWS, LANES))
            block = block.astype(jnp.int32).astype(short)
            rows = slice(cell * pitch + start, cell * pitch + start + ROWS)
            from_edge_ref[rows, :] = short_one_hot(across(block, 2 * count), edge_row)

    for start in range(0, slots, LANES):
        columns = slice(start, start + LANES)
        own_lane[:, columns], own_block[:, columns] = split_index(row_ref[:, columns] - count, short)
    w = w_ref[...]
    gather_columns(w, own_lane, own_block, None, functools.partial(store, values_ref))

    for cell in range(cells):
        for start in range(0, pitch, ROWS):
            block = jnp.broadcast_to(turned[start : start + ROWS, cell : cell + 1], (ROWS, LANES))
            block = block.astype(jnp.int32).astype(short)
            rows = slice(cell * pitch + start, cell * pitch + start + ROWS)
            from_own_ref[rows, :] = short_one_hot(across(block, owned), own_row)

    wide_ref[...] = jnp.zeros_like(wide_ref)
    copy.wait()
    for cell in range(cells):
        wide_ref[cell % 2, :nodes, :nodes] = matrix_ref[cell].astype(f32)
        padded_ref[cell] = wide_ref[cell % 2].astype(bf16)


def store(ref, rows, columns, values):
    ref[rows, columns] = values


def cell_block(values, matrix_ref, cell):
    pitch = matrix_ref.shape[1]
    return dot(values[:, cell * pitch : (cell + 1) * pitch], matrix_ref[cell])


def put_parts(parts_ref, cell, pitch, block):
    parts_ref[:, cell * pitch : (cell + 1) * pitch] = halves(block)


def chosen(flags_ref, first, second):
    even = flags_ref[2] > 0
    return jnp.where(even, second, first), jnp.where(even, first, second)


def cell_values(edge, inner_values_ref, edge_lane, edge_block, cell, pitch, before=0):
    tiles = []
    for start in range(cell * pitch, (cell + 1) * pitch, LANES):
        columns = slice(start, start + LANES)
        lane, block = edge_lane[:, columns], edge_block[:, columns]
        tiles.append(
            jnp.concatenate(
                [
                    gathered(
                        edge[row : row + ROWS], lane, block,
                        inner_values_ref[row : row + ROWS, columns], before,
                    )
                    for row in range(0, edge.shape[0], ROWS)
                ],
                axis=0,
            )
        )
    return jnp.concatenate(tiles, axis=1)


def send_sums(
    flags_ref, edge, inner_values_ref, edge_lane, edge_block, matrix_ref, from_edge_ref,
    parts_ref, first_ref, second_ref, before=0,
):
    cells, pitch, _ = matrix_ref.shape
    for cell in range(cells):
        values = cell_values(edge, inner_values_ref, edge_lane, edge_block, cell, pitch, before)
        parts_ref[:, cell * pitch : (cell + 1) * pitch] = halves(dot(values, matrix_ref[cell]))
    sums = joined(dot(parts_ref[...], from_edge_ref[...]))
    count = first_ref.shape[1]
    first_ref[...], second_ref[...] = chosen(flags_ref, sums[:, :count], sums[:, count:])


def first_kernel(
    flags_ref, inner_values_ref, got_first, got_second, own_lane, own_block, matrix_ref, from_edge_ref,
    parts_ref, first_ref, second_ref, state_ref,
):
    got, _ = chosen(flags_ref, got_first[...].astype(f32), got_second[...].astype(f32))
    got = jnp.where(flags_ref[0] > 0, got, jnp.zeros_like(got))
    state_ref[...] = got
    send_sums(
        flags_ref, got.astype(bf16), inner_values_ref, own_lane, own_block, matrix_ref, from_edge_ref,
        parts_ref, first_ref, second_ref, before=got.shape[1] // LANES,
    )


def advance(scale, applied, state, before):
    new = (applied - spectrum_center * state) * scale
    return new if before is None else new - before


def edge_step(scale, flags_ref, got_first, got_second, sum_first, sum_second, ghost, face, before):
    keep_ghost, keep_face = flags_ref[0] > 0, flags_ref[1] > 0
    got_ghost, got_face = chosen(flags_ref, got_first[...], got_second[...])
    sum_ghost, sum_face = chosen(flags_ref, sum_first[...], sum_second[...])
    applied_face = sum_face + jnp.where(keep_face, got_face, jnp.zeros_like(got_face))
    new_face = advance(scale, applied_face, face[...], before and before[1][...])
    new_ghost = advance(scale, sum_ghost + got_ghost, ghost[...], before and before[0][...])
    new_ghost = jnp.where(keep_ghost, new_ghost, jnp.zeros_like(new_ghost))
    return new_ghost, new_face


def edge_values(new_ghost, new_face):
    return jnp.concatenate([new_ghost.astype(bf16), new_face.astype(bf16)], axis=1)


def edge_kernel(scale, with_before, flags_ref, got_first, got_second, sum_first, sum_second, ghost, face, *rest):
    before, rest = (rest[:2], rest[2:]) if with_before else (None, rest)
    inner_values_ref, edge_lane, edge_block, matrix_ref, from_edge_ref, *outs = rest
    parts_ref, out_first, out_second, new_ghost, new_face = outs
    ghost_value, face_value = edge_step(
        scale, flags_ref, got_first, got_second, sum_first, sum_second, ghost, face, before
    )
    new_ghost[...] = ghost_value
    new_face[...] = face_value
    send_sums(
        flags_ref, edge_values(ghost_value, face_value), inner_values_ref, edge_lane, edge_block,
        matrix_ref, from_edge_ref, parts_ref, out_first, out_second,
    )


def start_kernel(
    scale, parts_ref, w_ref, face_ref, own_lane, own_block, from_own_ref,
    new_ref, values_ref, state_ref, inner_ref, node_lane, node_block, edge_lane, edge_block, table_ref,
):
    slots, owned = from_own_ref.shape
    count = face_ref.shape[1]
    half = ROWS // 2
    table_ref[...] = one_hot(lax.broadcasted_iota(jnp.int32, (owned, count), 0) == face_ref[...])
    order = lax.broadcasted_iota(jnp.int32, (half, count), 1)
    digits = jnp.concatenate([order >> 7, (order & (LANES - 1)) + 1], axis=0)
    sums = dot_rows(digits.astype(f32).astype(bf16), table_ref[...])

    applied = joined(dot(parts_ref[...], from_own_ref[...]))
    place = sums[:half] * float(LANES) + sums[half:]
    node_lane[...], node_block[...] = split_index(place.astype(jnp.int32) - 1, jnp.int32)
    inner = jnp.where(place > 0.5, 0.0, 1.0)
    inner_ref[...] = inner
    state = w_ref[...].astype(f32) * inner[:1]
    state_ref[...] = state
    new = advance(scale, applied, state, None) * inner[:1]
    new_ref[...] = new
    gather_columns(
        new.astype(bf16), own_lane, own_block, None, functools.partial(store, values_ref)
    )

    short_sums = sums.astype(bf16)
    for start in range(0, slots, LANES):
        columns = slice(start, start + LANES)
        at_face = gathered(short_sums, own_lane[:, columns], own_block[:, columns]).astype(f32)
        at_face = (at_face[:half] * float(LANES) + at_face[half:]).astype(jnp.int32)
        index = own_block[:half, columns].astype(jnp.int32) * LANES + own_lane[:half, columns].astype(jnp.int32)
        index = index + count
        index = jnp.where(index < count, index, jnp.where(at_face > 0, at_face + (count - 1), -1))
        lane, block = split_index(jnp.concatenate([index, index], axis=0), jnp.int16)
        edge_lane[:, columns] = lane
        edge_block[:, columns] = block


def inner_kernel(
    scale, parts_ref, state_ref, before_ref, own_lane, own_block, from_own_ref, inner_ref,
    new_ref, values_ref,
):
    applied = joined(dot(parts_ref[...], from_own_ref[...]))
    new = advance(scale, applied, state_ref[...], before_ref[...]) * inner_ref[:1]
    new_ref[...] = new
    gather_columns(
        new.astype(bf16), own_lane, own_block, None, functools.partial(store, values_ref)
    )


def density_kernel(
    flags_ref, got_first, got_second, sum_first, sum_second, ghost, face, before_ghost, before_face,
    inner_values_ref, edge_lane, edge_block, basis_ref, occupancy_ref,
    new_face, final_ref, at_ref, band_ref, *, scale, cells,
):
    ghost_value, face_value = edge_step(
        scale, flags_ref, got_first, got_second, sum_first, sum_second, ghost, face,
        (before_ghost, before_face),
    )
    new_face[...] = face_value
    edge = edge_values(ghost_value, face_value)
    nodes = basis_ref.shape[0]
    waves, slots = final_ref.shape
    pitch = slots // cells
    stacked = []
    for cell in range(cells):
        values = cell_values(edge, inner_values_ref, edge_lane, edge_block, cell, pitch)
        final_ref[:, cell * pitch : (cell + 1) * pitch] = values
        stacked.append(values)
    at = dot(jnp.concatenate(stacked, axis=0)[:, :nodes], basis_ref[...])
    at_ref[...] = at
    weights = column(occupancy_ref[...])
    for cell in range(cells):
        block = at[cell * waves : (cell + 1) * waves]
        band_ref[cell : cell + 1, :] = jnp.sum(weights * (block * block), axis=0, keepdims=True)


def products_kernel(
    values_ref, matrix_ref, basis_ref, product_ref, wide_basis_ref, wide_ref
):
    cells, pitch, _ = matrix_ref.shape
    values = values_ref[...]
    for cell in range(cells):
        product_ref[:, cell * pitch : (cell + 1) * pitch] = cell_block(values, matrix_ref, cell)
    nodes = basis_ref.shape[0]
    wide_ref[...] = jnp.zeros_like(wide_ref)
    wide_ref[:nodes, :] = basis_ref[...].astype(f32)
    wide_basis_ref[...] = wide_ref[...].astype(bf16)


def cube_root(x):
    return jnp.exp(jnp.log(x) * (1.0 / 3.0))


def exchange_correlation(density):
    radius = cube_root(0.75 / math.pi / density)
    exchange_part = -cube_root(3.0 / math.pi * density)
    shifted_radius = radius + 7.8
    correlation_part = -0.44 / shifted_radius - 0.44 * radius / (
        3.0 * shifted_radius * shifted_radius
    )
    return exchange_part + correlation_part


def potential_kernel(total_ref, *rest, factor):
    more, (core_ref, quad_ref, at_ref, basis_ref, product_ref, from_edge_ref,
           potential_ref, parts_ref, ghost_ref, twin_ref) = rest[:-10], rest[-10:]
    total = total_ref[...]
    if more:
        total = (total + more[0][...]) + (more[1][...] + more[2][...])
    potential = exchange_correlation(core_ref[...] + factor * total)
    potential_ref[...] = potential
    scaled = quad_ref[...] * potential
    cells = scaled.shape[0]
    waves, slots = product_ref.shape
    pitch = slots // cells
    weighted = jnp.concatenate(
        [
            (at_ref[cell * waves : (cell + 1) * waves, :] * scaled[cell : cell + 1]).astype(bf16)
            for cell in range(cells)
        ],
        axis=0,
    )
    projected = dot_rows(weighted, basis_ref[...])
    for cell in range(cells):
        block = product_ref[:, cell * pitch : (cell + 1) * pitch]
        put_parts(parts_ref, cell, pitch, block + projected[cell * waves : (cell + 1) * waves])
    count = ghost_ref.shape[1]
    sums = joined(dot(parts_ref[...], from_edge_ref[:, :count]))
    ghost_ref[...] = sums
    twin_ref[...] = sums


def residual_kernel(
    parts_ref, state_ref, face_ref, ritz_ref, from_own_ref, potential_ref,
    out_ref, shift_ref, potential_out, sem,
):
    copy = pltpu.make_async_copy(potential_ref, potential_out, sem)
    copy.start()
    ritz = column(ritz_ref[...])
    shift_ref[...] = ritz * face_ref[...]
    out_ref[...] = joined(dot(parts_ref[...], from_own_ref[...])) - ritz * state_ref[...]
    copy.wait()


def finish_kernel(
    flags_ref, got_first, got_second, partial_ref, shift_ref, node_lane, node_block,
    out_ref, hold_ref, sem,
):
    _, got = chosen(flags_ref, got_first[...], got_second[...])
    got = jnp.where(flags_ref[1] > 0, got, jnp.zeros_like(got)) - shift_ref[...]

    def add(rows, columns, values):
        hold_ref[rows, columns] = partial_ref[rows, columns] + values

    gather_columns(got, node_lane, node_block, None, add)
    copy = pltpu.make_async_copy(hold_ref, out_ref, sem)
    copy.start()
    copy.wait()


def paired(x, parity):
    domains, bands = lax.axis_size("space"), lax.axis_size("band")
    route = []
    for domain in range(domains):
        other = domain + 1 if domain % 2 == parity else domain - 1
        for band in range(bands):
            target = (other, band) if 0 <= other < domains else (domain, band ^ 1 if bands % 2 == 0 else band)
            route.append((domain * bands + band, target[0] * bands + target[1]))
    return lax.ppermute(x, ("space", "band"), route)


def exchanged(first, second):
    return paired(first, 0), paired(second, 1)


def swapped(x, axis, mask):
    return lax.ppermute(x, axis, [(i, i ^ mask) for i in range(lax.axis_size(axis))])


def band_parts(x, axis):
    count = lax.axis_size(axis)
    if count & (count - 1):
        return [lax.psum(x, axis)]
    bit = 1
    if count > 1:
        x = x + swapped(x, axis, bit)
        bit = 2
    parts = [x]
    while bit < count:
        x = parts[0] if len(parts) == 1 else (parts[0] + parts[1]) + (parts[2] + parts[3])
        if 2 * bit < count:
            parts = [x] + [swapped(x, axis, mask ^ 1) for mask in (bit, 2 * bit, 3 * bit)]
            bit *= 4
        else:
            parts = [x + swapped(x, axis, bit ^ 1)]
            bit *= 2
    return parts


def shards(
    wavefunctions,
    cell_hamiltonian,
    connectivity,
    face_nodes,
    basis_values,
    quad_weights,
    core_density,
    occupancy,
    ritz_values,
):
    waves, owned = wavefunctions.shape
    count = face_nodes.shape[0]
    cells, nodes = connectivity.shape
    points = basis_values.shape[1]
    pitch = -(-nodes // 128) * 128
    slots = cells * pitch
    band_total = waves * lax.axis_size("band")
    domain = lax.axis_index("space")
    flags = jnp.stack(
        [domain > 0, domain < lax.axis_size("space") - 1, domain % 2 == 0]
    ).astype(jnp.int32)
    edge_out = [((waves, count), f32)] * 2
    parts_out = ((2 * waves, slots), bf16)
    values_out = ((waves, slots), bf16)
    state_out = ((waves, owned), f32)

    index_out = ((ROWS, slots), jnp.int16)
    w, faces, links, start_face, start_twin = call(
        pick_kernel,
        [
            (wavefunctions.shape, bf16),
            ((1, count), jnp.int32),
            (connectivity.shape, jnp.int32),
            ((waves, count), bf16),
            ((waves, count), bf16),
        ],
        wavefunctions, face_nodes.reshape(1, count), connectivity,
        held=3, scratch=[pltpu.SemaphoreType.DMA((3,))], room=56,
    )
    start_pair = exchanged(start_twin, start_face)
    (
        from_own, from_edge, padded, own_lane, own_block, values
    ) = call(
        tables_kernel,
        [
            ((slots, owned), bf16),
            ((slots, 2 * count), bf16),
            ((cells, pitch, pitch), bf16),
            *[index_out] * 2,
            values_out,
        ],
        cell_hamiltonian, w, faces, links,
        held=1,
        scratch=[
            pltpu.VMEM((ROWS, slots), jnp.int32),
            pltpu.VMEM((-(-cells // LANES) * LANES, pitch), f32),
            pltpu.VMEM((2, pitch, pitch), f32),
            pltpu.VMEM(cell_hamiltonian.shape, bf16),
            pltpu.SemaphoreType.DMA,
        ],
        room=44,
    )
    parts, *sums, ghost = call(
        first_kernel,
        [parts_out, *edge_out, edge_out[0]],
        flags, values, *start_pair, own_lane, own_block, padded, from_edge, smem=1,
    )
    face = start_face.astype(f32)
    before_edge = ()
    scale = 1.0 / spectrum_half
    for step in range(3):
        got = exchanged(*sums)
        if step == 0:
            (
                new_state, values, state, inner, node_lane, node_block, edge_lane, edge_block
            ) = call(
                functools.partial(start_kernel, scale),
                [
                    state_out,
                    values_out,
                    state_out,
                    ((ROWS // 2, owned), f32),
                    ((ROWS // 2, owned), jnp.int32),
                    ((ROWS // 2, owned), jnp.int32),
                    *[index_out] * 2,
                ],
                parts, w, faces, own_lane, own_block, from_own,
                scratch=[pltpu.VMEM((owned, count), bf16)],
            )
        else:
            new_state, values = call(
                functools.partial(inner_kernel, scale),
                [state_out, values_out],
                parts, state, before_state, own_lane, own_block, from_own, inner,
            )
        received = (flags, *got, *sums, ghost, face, *before_edge)
        if step < 2:
            parts, *sums, new_ghost, new_face = call(
                functools.partial(edge_kernel, scale, step > 0),
                [parts_out, *edge_out, *edge_out],
                *received, values, edge_lane, edge_block, padded, from_edge, smem=1,
            )
            before_edge, ghost, face = (ghost, face), new_ghost, new_face
        else:
            face, final, at, band = call(
                functools.partial(density_kernel, scale=scale, cells=cells),
                [edge_out[0], values_out, ((cells * waves, points), f32), ((cells, points), f32)],
                *received, values, edge_lane, edge_block, basis_values, occupancy.reshape(1, waves), smem=1,
            )
        before_state, state = state, new_state
        scale = 2.0 / spectrum_half
    products, wide_basis = call(
        products_kernel,
        [((waves, slots), f32), ((pitch, points), bf16)],
        final, padded, basis_values, scratch=[pltpu.VMEM((pitch, points), f32)],
    )
    totals = band_parts(band, "band")
    potential, parts, *sums = call(
        functools.partial(potential_kernel, factor=2.0 / band_total),
        [((cells, points), f32), parts_out, *edge_out],
        *totals, core_density, quad_weights, at, wide_basis, products, from_edge,
    )
    returned = exchanged(*sums)
    partial, shift, potential = call(
        residual_kernel,
        [state_out, edge_out[0], ((cells, points), f32)],
        parts, state, face, ritz_values.reshape(1, waves), from_own, potential,
        sent=1, scratch=[pltpu.SemaphoreType.DMA],
    )
    (residual,) = call(
        finish_kernel, [state_out], flags, *returned, partial, shift, node_lane, node_block,
        smem=1, sent=1, scratch=[pltpu.VMEM(*state_out), pltpu.SemaphoreType.DMA],
    )
    return (residual, potential)


def solution(mesh):
    in_specs = (
        P("band", "space"),
        P("space", None, None),
        P("space", None),
        P("space"),
        P(),
        P("space", None),
        P("space", None),
        P("band"),
        P("band"),
    )
    out_specs = (P("band", "space"), P("space", None))
    return jax.shard_map(shards, mesh=mesh, in_specs=in_specs, out_specs=out_specs, check_vma=False)
```

```python
import functools
import math

import jax
import jax.numpy as jnp
from jax import lax
from jax.experimental import pallas as pl
from jax.experimental.pallas import tpu as pltpu
from jax.sharding import PartitionSpec as P

spectrum_center = 5.0
spectrum_half = 5.5

VMEM = pl.BlockSpec(memory_space=pltpu.VMEM)
SMEM = pl.BlockSpec(memory_space=pltpu.SMEM)
OUTSIDE = pl.BlockSpec(memory_space=pltpu.HBM)
bf16 = jnp.bfloat16
f32 = jnp.float32


def dot(left, right):
    return jnp.dot(left, right, preferred_element_type=f32)


def dot_rows(left, right):
    return lax.dot_general(left, right, (((1,), (1,)), ((), ())), preferred_element_type=f32)


def halves(x):
    high = x.astype(bf16)
    low = (x - high.astype(f32)).astype(bf16)
    return jnp.concatenate([high, low], axis=0)


def joined(x):
    rows = x.shape[0] // 2
    return x[:rows] + x[rows:]


def column(row):
    n = row.shape[1]
    eye = lax.broadcasted_iota(jnp.int32, (n, n), 0) == lax.broadcasted_iota(jnp.int32, (n, n), 1)
    return jnp.sum(jnp.where(eye, row, jnp.zeros_like(row)), axis=1, keepdims=True)


def one_hot(hit):
    return jnp.where(hit, 1.0, 0.0).astype(bf16)


def call(kernel, outs, *args, flops=1 << 28, smem=0, held=0, sent=0, scratch=(), room=20):
    count = len(args) - smem - held
    kept = len(outs) - sent
    return pl.pallas_call(
        kernel,
        out_shape=[pltpu.VMEM(*out) for out in outs[:kept]]
        + [jax.ShapeDtypeStruct(*out) for out in outs[kept:]],
        in_specs=[SMEM] * smem + [OUTSIDE] * held + [VMEM] * count,
        out_specs=[VMEM] * kept + [OUTSIDE] * sent,
        scratch_shapes=list(scratch),
        compiler_params=pltpu.CompilerParams(vmem_limit_bytes=room << 20),
        cost_estimate=pl.CostEstimate(flops=flops, bytes_accessed=1 << 20, transcendentals=0),
    )(*args)


LANES = 128
ROWS = 16
ALONG = lax.GatherDimensionNumbers(
    offset_dims=(),
    collapsed_slice_dims=(1,),
    start_index_map=(1,),
    operand_batching_dims=(0,),
    start_indices_batching_dims=(0,),
)


def along(block, lane):
    return lax.gather(
        block, lane[..., None], ALONG, slice_sizes=(1, 1),
        mode=lax.GatherScatterMode.PROMISE_IN_BOUNDS,
    )


def gathered(source, lane, block, start=None, before=0):
    out = jnp.zeros(lane.shape, source.dtype) if start is None else start
    for number in range(source.shape[1] // LANES):
        part = along(source[:, number * LANES : (number + 1) * LANES], lane)
        out = jnp.where(block == number - before, part, out)
    return out


def gather_columns(source, lane_ref, block_ref, start, put):
    rows = lane_ref.shape[0]
    for column_start in range(0, lane_ref.shape[1], LANES):
        columns = slice(column_start, column_start + LANES)
        lane, block = lane_ref[:, columns], block_ref[:, columns]
        for row in range(0, source.shape[0], rows):
            begin = None if start is None else start[row : row + rows, columns]
            put(slice(row, row + rows), columns, gathered(source[row : row + rows], lane, block, begin))


def split_index(index, dtype):
    return (index & (LANES - 1)).astype(dtype), (index >> 7).astype(dtype)


def pick_kernel(
    w_in, face_in, links_in, matrix_in, w_ref, face_ref, links_ref, out_ref, twin_ref, matrix_ref, sems
):
    pairs = ((w_in, w_ref), (face_in, face_ref), (links_in, links_ref), (matrix_in, matrix_ref))
    copies = [
        pltpu.make_async_copy(source, target, sems.at[i]) for i, (source, target) in enumerate(pairs)
    ]
    for copy in copies:
        copy.start()
    for copy in copies[:2]:
        copy.wait()
    count = face_ref.shape[1]
    w = w_ref[...]
    for start in range(0, count, LANES):
        index = jnp.broadcast_to(face_ref[:, start : start + LANES], (ROWS, LANES))
        lane, block = split_index(index, jnp.int16)
        for row in range(0, w.shape[0], ROWS):
            picked = gathered(w[row : row + ROWS], lane, block)
            out_ref[row : row + ROWS, start : start + LANES] = picked
            twin_ref[row : row + ROWS, start : start + LANES] = picked
    for copy in copies[2:]:
        copy.wait()


def short_one_hot(left, right):
    return jnp.where(left == right, jnp.ones(left.shape, bf16), jnp.zeros(left.shape, bf16))


def across(block, width):
    return jnp.concatenate([block] * (width // block.shape[1]), axis=1)


def tables_kernel(
    w_ref, face_ref, links_ref,
    from_own_ref, from_edge_ref, own_lane, own_block, values_ref,
    row_ref, turn_ref,
):
    slots, owned = from_own_ref.shape
    count = face_ref.shape[1]
    cells, nodes = links_ref.shape
    pitch = slots // cells
    short = jnp.int16

    row_ref[...] = jnp.full(row_ref.shape, -1, jnp.int32)
    turn_ref[...] = jnp.full(turn_ref.shape, -1.0, f32)
    for cell in range(cells):
        line = links_ref[cell : cell + 1, :]
        row_ref[:, cell * pitch : cell * pitch + nodes] = jnp.broadcast_to(line, (ROWS, nodes))
        turn_ref[cell : cell + 1, :nodes] = line.astype(f32)

    edge_row = jnp.concatenate(
        [
            lax.broadcasted_iota(jnp.int32, (ROWS, count), 1),
            jnp.broadcast_to(face_ref[...], (ROWS, count)) + count,
        ],
        axis=1,
    ).astype(short)
    own_row = (lax.broadcasted_iota(jnp.int32, (ROWS, owned), 1) + count).astype(short)
    turned = jnp.transpose(turn_ref[...])
    for cell in range(cells):
        for start in range(0, pitch, ROWS):
            block = jnp.broadcast_to(turned[start : start + ROWS, cell : cell + 1], (ROWS, LANES))
            block = block.astype(jnp.int32).astype(short)
            rows = slice(cell * pitch + start, cell * pitch + start + ROWS)
            from_edge_ref[rows, :] = short_one_hot(across(block, 2 * count), edge_row)

    for start in range(0, slots, LANES):
        columns = slice(start, start + LANES)
        own_lane[:, columns], own_block[:, columns] = split_index(row_ref[:, columns] - count, short)
    w = w_ref[...]
    gather_columns(w, own_lane, own_block, None, functools.partial(store, values_ref))

    for cell in range(cells):
        for start in range(0, pitch, ROWS):
            block = jnp.broadcast_to(turned[start : start + ROWS, cell : cell + 1], (ROWS, LANES))
            block = block.astype(jnp.int32).astype(short)
            rows = slice(cell * pitch + start, cell * pitch + start + ROWS)
            from_own_ref[rows, :] = short_one_hot(across(block, owned), own_row)


def store(ref, rows, columns, values):
    ref[rows, columns] = values


def put_parts(parts_ref, cell, pitch, block):
    parts_ref[:, cell * pitch : (cell + 1) * pitch] = halves(block)


def chosen(flags_ref, first, second):
    even = flags_ref[2] > 0
    return jnp.where(even, second, first), jnp.where(even, first, second)


def cell_values(edge, inner_values_ref, edge_lane, edge_block, cell, pitch, before=0):
    tiles = []
    for start in range(cell * pitch, (cell + 1) * pitch, LANES):
        columns = slice(start, start + LANES)
        lane, block = edge_lane[:, columns], edge_block[:, columns]
        tiles.append(
            jnp.concatenate(
                [
                    gathered(
                        edge[row : row + ROWS], lane, block,
                        inner_values_ref[row : row + ROWS, columns], before,
                    )
                    for row in range(0, edge.shape[0], ROWS)
                ],
                axis=0,
            )
        )
    return jnp.concatenate(tiles, axis=1)


def send_sums(
    flags_ref, edge, inner_values_ref, edge_lane, edge_block, matrix_ref, from_edge_ref,
    parts_ref, first_ref, second_ref, before=0,
):
    cells, nodes, _ = matrix_ref.shape
    pitch = parts_ref.shape[1] // cells
    for cell in range(cells):
        values = cell_values(edge, inner_values_ref, edge_lane, edge_block, cell, pitch, before)
        tail = slice((cell + 1) * pitch - LANES, (cell + 1) * pitch)
        parts_ref[:, tail] = jnp.zeros((parts_ref.shape[0], LANES), bf16)
        columns = slice(cell * pitch, cell * pitch + nodes)
        parts_ref[:, columns] = halves(dot(values[:, :nodes], matrix_ref[cell]))
    sums = joined(dot(parts_ref[...], from_edge_ref[...]))
    count = first_ref.shape[1]
    first_ref[...], second_ref[...] = chosen(flags_ref, sums[:, :count], sums[:, count:])


def first_kernel(
    flags_ref, inner_values_ref, got_first, got_second, own_lane, own_block, matrix_ref, from_edge_ref,
    parts_ref, first_ref, second_ref, state_ref,
):
    got, _ = chosen(flags_ref, got_first[...].astype(f32), got_second[...].astype(f32))
    got = jnp.where(flags_ref[0] > 0, got, jnp.zeros_like(got))
    state_ref[...] = got
    send_sums(
        flags_ref, got.astype(bf16), inner_values_ref, own_lane, own_block, matrix_ref, from_edge_ref,
        parts_ref, first_ref, second_ref, before=got.shape[1] // LANES,
    )


def advance(scale, applied, state, before):
    new = (applied - spectrum_center * state) * scale
    return new if before is None else new - before


def edge_step(scale, flags_ref, got_first, got_second, sum_first, sum_second, ghost, face, before):
    keep_ghost, keep_face = flags_ref[0] > 0, flags_ref[1] > 0
    got_ghost, got_face = chosen(flags_ref, got_first[...], got_second[...])
    sum_ghost, sum_face = chosen(flags_ref, sum_first[...], sum_second[...])
    applied_face = sum_face + jnp.where(keep_face, got_face, jnp.zeros_like(got_face))
    new_face = advance(scale, applied_face, face[...], before and before[1][...])
    new_ghost = advance(scale, sum_ghost + got_ghost, ghost[...], before and before[0][...])
    new_ghost = jnp.where(keep_ghost, new_ghost, jnp.zeros_like(new_ghost))
    return new_ghost, new_face


def edge_values(new_ghost, new_face):
    return jnp.concatenate([new_ghost.astype(bf16), new_face.astype(bf16)], axis=1)


def edge_kernel(scale, with_before, flags_ref, got_first, got_second, sum_first, sum_second, ghost, face, *rest):
    before, rest = (rest[:2], rest[2:]) if with_before else (None, rest)
    inner_values_ref, edge_lane, edge_block, matrix_ref, from_edge_ref, *outs = rest
    parts_ref, out_first, out_second, new_ghost, new_face = outs
    ghost_value, face_value = edge_step(
        scale, flags_ref, got_first, got_second, sum_first, sum_second, ghost, face, before
    )
    new_ghost[...] = ghost_value
    new_face[...] = face_value
    send_sums(
        flags_ref, edge_values(ghost_value, face_value), inner_values_ref, edge_lane, edge_block,
        matrix_ref, from_edge_ref, parts_ref, out_first, out_second,
    )


def start_kernel(
    scale, parts_ref, w_ref, face_ref, own_lane, own_block, from_own_ref,
    new_ref, values_ref, state_ref, inner_ref, node_lane, node_block, edge_lane, edge_block, table_ref,
):
    slots, owned = from_own_ref.shape
    count = face_ref.shape[1]
    half = ROWS // 2
    table_ref[...] = one_hot(lax.broadcasted_iota(jnp.int32, (owned, count), 0) == face_ref[...])
    order = lax.broadcasted_iota(jnp.int32, (half, count), 1)
    digits = jnp.concatenate([order >> 7, (order & (LANES - 1)) + 1], axis=0)
    sums = dot_rows(digits.astype(f32).astype(bf16), table_ref[...])

    applied = joined(dot(parts_ref[...], from_own_ref[...]))
    place = sums[:half] * float(LANES) + sums[half:]
    node_lane[...], node_block[...] = split_index(place.astype(jnp.int32) - 1, jnp.int32)
    inner = jnp.where(place > 0.5, 0.0, 1.0)
    inner_ref[...] = inner
    state = w_ref[...].astype(f32) * inner[:1]
    state_ref[...] = state
    new = advance(scale, applied, state, None) * inner[:1]
    new_ref[...] = new
    gather_columns(
        new.astype(bf16), own_lane, own_block, None, functools.partial(store, values_ref)
    )

    short_sums = sums.astype(bf16)
    for start in range(0, slots, LANES):
        columns = slice(start, start + LANES)
        at_face = gathered(short_sums, own_lane[:, columns], own_block[:, columns]).astype(f32)
        at_face = (at_face[:half] * float(LANES) + at_face[half:]).astype(jnp.int32)
        index = own_block[:half, columns].astype(jnp.int32) * LANES + own_lane[:half, columns].astype(jnp.int32)
        index = index + count
        index = jnp.where(index < count, index, jnp.where(at_face > 0, at_face + (count - 1), -1))
        lane, block = split_index(jnp.concatenate([index, index], axis=0), jnp.int16)
        edge_lane[:, columns] = lane
        edge_block[:, columns] = block


def inner_kernel(
    scale, parts_ref, state_ref, before_ref, own_lane, own_block, from_own_ref, inner_ref,
    new_ref, values_ref,
):
    applied = joined(dot(parts_ref[...], from_own_ref[...]))
    new = advance(scale, applied, state_ref[...], before_ref[...]) * inner_ref[:1]
    new_ref[...] = new
    gather_columns(
        new.astype(bf16), own_lane, own_block, None, functools.partial(store, values_ref)
    )


def density_kernel(
    flags_ref, got_first, got_second, sum_first, sum_second, ghost, face, before_ghost, before_face,
    inner_values_ref, edge_lane, edge_block, basis_ref, occupancy_ref,
    new_face, final_ref, at_ref, band_ref, *, scale, cells,
):
    ghost_value, face_value = edge_step(
        scale, flags_ref, got_first, got_second, sum_first, sum_second, ghost, face,
        (before_ghost, before_face),
    )
    new_face[...] = face_value
    edge = edge_values(ghost_value, face_value)
    nodes = basis_ref.shape[0]
    waves, slots = final_ref.shape
    pitch = slots // cells
    stacked = []
    for cell in range(cells):
        values = cell_values(edge, inner_values_ref, edge_lane, edge_block, cell, pitch)
        final_ref[:, cell * pitch : (cell + 1) * pitch] = values
        stacked.append(values)
    at = dot(jnp.concatenate(stacked, axis=0)[:, :nodes], basis_ref[...])
    at_ref[...] = at
    weights = column(occupancy_ref[...])
    for cell in range(cells):
        block = at[cell * waves : (cell + 1) * waves]
        band_ref[cell : cell + 1, :] = jnp.sum(weights * (block * block), axis=0, keepdims=True)


def products_kernel(
    values_ref, matrix_ref, basis_ref, product_ref, wide_basis_ref, wide_ref
):
    cells, nodes, _ = matrix_ref.shape
    pitch = product_ref.shape[1] // cells
    product_ref[...] = jnp.zeros_like(product_ref)
    for cell in range(cells):
        columns = slice(cell * pitch, cell * pitch + nodes)
        product_ref[:, columns] = dot(values_ref[:, columns], matrix_ref[cell])
    nodes = basis_ref.shape[0]
    wide_ref[...] = jnp.zeros_like(wide_ref)
    wide_ref[:nodes, :] = basis_ref[...].astype(f32)
    wide_basis_ref[...] = wide_ref[...].astype(bf16)


def cube_root(x):
    return jnp.exp(jnp.log(x) * (1.0 / 3.0))


def exchange_correlation(density):
    radius = cube_root(0.75 / math.pi / density)
    exchange_part = -cube_root(3.0 / math.pi * density)
    shifted_radius = radius + 7.8
    correlation_part = -0.44 / shifted_radius - 0.44 * radius / (
        3.0 * shifted_radius * shifted_radius
    )
    return exchange_part + correlation_part


def potential_kernel(total_ref, *rest, factor):
    more, (core_ref, quad_ref, at_ref, basis_ref, product_ref, from_edge_ref,
           potential_ref, parts_ref, ghost_ref, twin_ref) = rest[:-10], rest[-10:]
    total = total_ref[...]
    if more:
        total = (total + more[0][...]) + (more[1][...] + more[2][...])
    potential = exchange_correlation(core_ref[...] + factor * total)
    potential_ref[...] = potential
    scaled = quad_ref[...] * potential
    cells = scaled.shape[0]
    waves, slots = product_ref.shape
    pitch = slots // cells
    weighted = jnp.concatenate(
        [
            (at_ref[cell * waves : (cell + 1) * waves, :] * scaled[cell : cell + 1]).astype(bf16)
            for cell in range(cells)
        ],
        axis=0,
    )
    projected = dot_rows(weighted, basis_ref[...])
    for cell in range(cells):
        block = product_ref[:, cell * pitch : (cell + 1) * pitch]
        put_parts(parts_ref, cell, pitch, block + projected[cell * waves : (cell + 1) * waves])
    count = ghost_ref.shape[1]
    sums = joined(dot(parts_ref[...], from_edge_ref[:, :count]))
    ghost_ref[...] = sums
    twin_ref[...] = sums


def residual_kernel(
    parts_ref, state_ref, face_ref, ritz_ref, from_own_ref, potential_ref,
    out_ref, shift_ref, potential_out, sem,
):
    copy = pltpu.make_async_copy(potential_ref, potential_out, sem)
    copy.start()
    ritz = column(ritz_ref[...])
    shift_ref[...] = ritz * face_ref[...]
    out_ref[...] = joined(dot(parts_ref[...], from_own_ref[...])) - ritz * state_ref[...]
    copy.wait()


def finish_kernel(
    flags_ref, got_first, got_second, partial_ref, shift_ref, node_lane, node_block,
    out_ref, hold_ref, sem,
):
    _, got = chosen(flags_ref, got_first[...], got_second[...])
    got = jnp.where(flags_ref[1] > 0, got, jnp.zeros_like(got)) - shift_ref[...]

    def add(rows, columns, values):
        hold_ref[rows, columns] = partial_ref[rows, columns] + values

    gather_columns(got, node_lane, node_block, None, add)
    copy = pltpu.make_async_copy(hold_ref, out_ref, sem)
    copy.start()
    copy.wait()


def paired(x, parity):
    domains, bands = lax.axis_size("space"), lax.axis_size("band")
    route = []
    for domain in range(domains):
        other = domain + 1 if domain % 2 == parity else domain - 1
        for band in range(bands):
            target = (other, band) if 0 <= other < domains else (domain, band ^ 1 if bands % 2 == 0 else band)
            route.append((domain * bands + band, target[0] * bands + target[1]))
    return lax.ppermute(x, ("space", "band"), route)


def exchanged(first, second):
    return paired(first, 0), paired(second, 1)


def swapped(x, axis, mask):
    return lax.ppermute(x, axis, [(i, i ^ mask) for i in range(lax.axis_size(axis))])


def band_parts(x, axis):
    count = lax.axis_size(axis)
    if count & (count - 1):
        return [lax.psum(x, axis)]
    bit = 1
    if count > 1:
        x = x + swapped(x, axis, bit)
        bit = 2
    parts = [x]
    while bit < count:
        x = parts[0] if len(parts) == 1 else (parts[0] + parts[1]) + (parts[2] + parts[3])
        if 2 * bit < count:
            parts = [x] + [swapped(x, axis, mask ^ 1) for mask in (bit, 2 * bit, 3 * bit)]
            bit *= 4
        else:
            parts = [x + swapped(x, axis, bit ^ 1)]
            bit *= 2
    return parts


def shards(
    wavefunctions,
    cell_hamiltonian,
    connectivity,
    face_nodes,
    basis_values,
    quad_weights,
    core_density,
    occupancy,
    ritz_values,
):
    waves, owned = wavefunctions.shape
    count = face_nodes.shape[0]
    cells, nodes = connectivity.shape
    points = basis_values.shape[1]
    pitch = -(-nodes // 128) * 128
    slots = cells * pitch
    band_total = waves * lax.axis_size("band")
    domain = lax.axis_index("space")
    flags = jnp.stack(
        [domain > 0, domain < lax.axis_size("space") - 1, domain % 2 == 0]
    ).astype(jnp.int32)
    edge_out = [((waves, count), f32)] * 2
    parts_out = ((2 * waves, slots), bf16)
    values_out = ((waves, slots), bf16)
    state_out = ((waves, owned), f32)

    index_out = ((ROWS, slots), jnp.int16)
    w, faces, links, start_face, start_twin, matrix = call(
        pick_kernel,
        [
            (wavefunctions.shape, bf16),
            ((1, count), jnp.int32),
            (connectivity.shape, jnp.int32),
            ((waves, count), bf16),
            ((waves, count), bf16),
            (cell_hamiltonian.shape, bf16),
        ],
        wavefunctions, face_nodes.reshape(1, count), connectivity, cell_hamiltonian,
        held=4, scratch=[pltpu.SemaphoreType.DMA((4,))], room=56,
    )
    start_pair = exchanged(start_twin, start_face)
    (
        from_own, from_edge, own_lane, own_block, values
    ) = call(
        tables_kernel,
        [
            ((slots, owned), bf16),
            ((slots, 2 * count), bf16),
            *[index_out] * 2,
            values_out,
        ],
        w, faces, links,
        scratch=[
            pltpu.VMEM((ROWS, slots), jnp.int32),
            pltpu.VMEM((-(-cells // LANES) * LANES, pitch), f32),
        ],
    )
    parts, *sums, ghost = call(
        first_kernel,
        [parts_out, *edge_out, edge_out[0]],
        flags, values, *start_pair, own_lane, own_block, matrix, from_edge, smem=1,
    )
    face = start_face.astype(f32)
    before_edge = ()
    scale = 1.0 / spectrum_half
    for step in range(3):
        got = exchanged(*sums)
        if step == 0:
            (
                new_state, values, state, inner, node_lane, node_block, edge_lane, edge_block
            ) = call(
                functools.partial(start_kernel, scale),
                [
                    state_out,
                    values_out,
                    state_out,
                    ((ROWS // 2, owned), f32),
                    ((ROWS // 2, owned), jnp.int32),
                    ((ROWS // 2, owned), jnp.int32),
                    *[index_out] * 2,
                ],
                parts, w, faces, own_lane, own_block, from_own,
                scratch=[pltpu.VMEM((owned, count), bf16)],
            )
        else:
            new_state, values = call(
                functools.partial(inner_kernel, scale),
                [state_out, values_out],
                parts, state, before_state, own_lane, own_block, from_own, inner,
            )
        received = (flags, *got, *sums, ghost, face, *before_edge)
        if step < 2:
            parts, *sums, new_ghost, new_face = call(
                functools.partial(edge_kernel, scale, step > 0),
                [parts_out, *edge_out, *edge_out],
                *received, values, edge_lane, edge_block, matrix, from_edge, smem=1,
            )
            before_edge, ghost, face = (ghost, face), new_ghost, new_face
        else:
            face, final, at, band = call(
                functools.partial(density_kernel, scale=scale, cells=cells),
                [edge_out[0], values_out, ((cells * waves, points), f32), ((cells, points), f32)],
                *received, values, edge_lane, edge_block, basis_values, occupancy.reshape(1, waves), smem=1,
            )
        before_state, state = state, new_state
        scale = 2.0 / spectrum_half
    products, wide_basis = call(
        products_kernel,
        [((waves, slots), f32), ((pitch, points), bf16)],
        final, matrix, basis_values, scratch=[pltpu.VMEM((pitch, points), f32)],
    )
    totals = band_parts(band, "band")
    potential, parts, *sums = call(
        functools.partial(potential_kernel, factor=2.0 / band_total),
        [((cells, points), f32), parts_out, *edge_out],
        *totals, core_density, quad_weights, at, wide_basis, products, from_edge,
    )
    returned = exchanged(*sums)
    partial, shift, potential = call(
        residual_kernel,
        [state_out, edge_out[0], ((cells, points), f32)],
        parts, state, face, ritz_values.reshape(1, waves), from_own, potential,
        sent=1, scratch=[pltpu.SemaphoreType.DMA],
    )
    (residual,) = call(
        finish_kernel, [state_out], flags, *returned, partial, shift, node_lane, node_block,
        smem=1, sent=1, scratch=[pltpu.VMEM(*state_out), pltpu.SemaphoreType.DMA],
    )
    return (residual, potential)


def solution(mesh):
    in_specs = (
        P("band", "space"),
        P("space", None, None),
        P("space", None),
        P("space"),
        P(),
        P("space", None),
        P("space", None),
        P("band"),
        P("band"),
    )
    out_specs = (P("band", "space"), P("space", None))
    return jax.shard_map(shards, mesh=mesh, in_specs=in_specs, out_specs=out_specs, check_vma=False)
```
